32 devices in a mesh: dp: 4 (over y, x), expert: 8 (over z, core).
Axes of the slice: x: 2, y: 2, z: 4, core: 2. Of those that a mesh axis runs over, the one named last changes fastest.
Arguments:
- layer_input: bfloat16 [4096, 640], P(('dp', 'expert')), may hold values from -6 to 6
- output_grad: bfloat16 [4096, 640], P(('dp', 'expert')), may hold values from -6 to 6
- gate_weights: float32 [4096, 2], P(('dp', 'expert')), may hold values from 0.1 to 1
- expert_ids: int32 [4096, 2], P(('dp', 'expert')), may hold values from 0 to 7, as said below
- slot_positions: int32 [4096, 2], P(('dp', 'expert')), may hold values from 0 to 23, as said below
- keep_mask: int32 [4096, 2], P(('dp', 'expert')), may hold values from 0 to 1, as said below
- weight_in: bfloat16 [8, 640, 5120], P('expert', None, 'dp'), may hold values from -0.25 to 0.25
- weight_out: bfloat16 [8, 5120, 640], P('expert', 'dp'), may hold values from -0.078125 to 0.078125
Outputs:
- input_grad: bfloat16 [4096, 640], P(('dp', 'expert'))
- weight_in_grad: bfloat16 [8, 640, 5120], P('expert', None, 'dp')
- weight_out_grad: bfloat16 [8, 5120, 640], P('expert', 'dp')
The draws below stay inside these ranges and needn't reach their ends.
Inputs may be any that keep to these rules, and one draw needn't show every extreme that they name: `expert_ids`: a token's two experts differ. `slot_positions`: within the tokens of one device, taken in order with a token's first choice before its second, the choices naming one expert take positions 0, 1, 2 and so on; a choice at position 24 or beyond is dropped and has slot 0; kept choices of one device and expert have distinct slots. `keep_mask`: 1 exactly where the choice's position is below 24.
All inputs are finite; a program needn't handle non-finite values.
Results may differ from the reference program's by a relative error of at most 0.015.
Values may be sent and summed in bfloat16 or wider, within the bound.
No kernel may reach another device: no remote copies, remote signals or barrier semaphores. Data moves between devices by JAX's collectives and lax.ppermute only.
A program may use at most 64 MiB of HBM per device.

```python
import jax
import jax.numpy as jnp
from jax import lax

D = 640
FF = 5120
TOK_DEV = 128
EXPERTS = 8
CAP = 24
TOKENS = 4096
N_DP = 4


def routing_table(key):
    blocks = TOKENS // TOK_DEV
    key_hot = jax.random.fold_in(key, 11)
    key_choose = jax.random.fold_in(key, 12)
    key_first = jax.random.fold_in(key, 13)
    key_offset = jax.random.fold_in(key, 14)
    hot_expert = jax.random.randint(key_hot, (blocks,), 0, EXPERTS, dtype=jnp.int32)
    hot_tokens = jnp.repeat(hot_expert, TOK_DEV)
    choose = jax.random.randint(key_choose, (TOKENS,), 0, 4, dtype=jnp.int32)
    random_first = jax.random.randint(key_first, (TOKENS,), 0, EXPERTS, dtype=jnp.int32)
    first_pick = jnp.where(choose == 0, hot_tokens, random_first)
    offset = jax.random.randint(key_offset, (TOKENS,), 1, EXPERTS, dtype=jnp.int32)
    second = (first_pick + offset) % EXPERTS
    chosen = jnp.stack([first_pick, second], axis=1).astype(jnp.int32)
    flat_choice = chosen.reshape(blocks, 2 * TOK_DEV)
    onehot = (flat_choice[:, :, None] == jnp.arange(EXPERTS, dtype=jnp.int32)[None, None, :]).astype(jnp.int32)
    earlier = jnp.cumsum(onehot, axis=1) - onehot
    position = jnp.sum(earlier * onehot, axis=2).reshape(TOKENS, 2)
    keeping = (position < CAP).astype(jnp.int32)
    slots = jnp.where(position < CAP, position, 0).astype(jnp.int32)
    return (chosen, slots, keeping)


def draw_expert_ids(key, part):
    return routing_table(key)[0]


def draw_slot_positions(key, part):
    return routing_table(key)[1]


def draw_keep_mask(key, part):
    return routing_table(key)[2]


def block_levels(key, shape, shards, low, high):
    loudness, own = 1.0, jax.random.fold_in(key, 6)
    for dim, shards_of in shards:
        steps = jnp.exp(jax.random.uniform(jax.random.fold_in(own, dim), (shards_of,), jnp.float32, low / len(shards), high / len(shards)))
        loudness = loudness * jnp.repeat(steps, shape[dim] // shards_of).reshape([-1 if axis == dim else 1 for axis in range(len(shape))])
    return loudness


def bell_draw(rng, dims, scale, bound, shards=(), kind=jnp.bfloat16):
    values = jax.random.normal(rng, dims, jnp.float32) * scale
    if len(shards) > 0:
        values = block_levels(rng, dims, shards, -0.22, 0.18) * values
    return jnp.clip(values, min=-bound, max=bound).astype(kind)


def setup_inputs(seed: int = 0) -> dict:
    streams_of = jax.random.split(jax.random.key(seed), 9)
    layer_input = bell_draw(streams_of[0], (TOKENS, D), 1.0, 6.0, ((0, 32),))
    output_grad = bell_draw(streams_of[1], (TOKENS, D), 1.0, 6.0, ((0, 32),))
    gate_weights = jnp.clip(0.1 + 0.9 * jax.random.uniform(streams_of[2], (TOKENS, 2), jnp.float32) ** block_levels(streams_of[2], (TOKENS, 2), ((0, 32),), -0.2, 0.2), 0.1, 1.0)
    expert_ids = draw_expert_ids(jax.random.fold_in(streams_of[8], 71), 0)
    slot_positions = draw_slot_positions(jax.random.fold_in(streams_of[8], 71), 0)
    keep_mask = draw_keep_mask(jax.random.fold_in(streams_of[8], 71), 0)
    weight_in = bell_draw(streams_of[6], (EXPERTS, D, FF), D ** -0.5, 0.25, ((0, 8), (2, 4)))
    weight_out = bell_draw(streams_of[7], (EXPERTS, FF, D), FF ** -0.5, 0.078125, ((0, 8), (1, 4)))
    return dict(layer_input=layer_input, output_grad=output_grad, gate_weights=gate_weights, expert_ids=expert_ids, slot_positions=slot_positions, keep_mask=keep_mask, weight_in=weight_in, weight_out=weight_out)


root_coef = 0.7978845608028654
cube_coef = 0.044715


def gelu_value(preact):
    inner_arg = root_coef * (preact + cube_coef * preact * preact * preact)
    return 0.5 * preact * (1.0 + jnp.tanh(inner_arg))


def gelu_slope(preact):
    inner_arg = root_coef * (preact + cube_coef * preact * preact * preact)
    tanh_value = jnp.tanh(inner_arg)
    return 0.5 * (1.0 + tanh_value) + 0.5 * preact * (1.0 - tanh_value * tanh_value) * root_coef * (1.0 + 3.0 * cube_coef * preact * preact)


def expert_backward(operands):
    rows_in, rows_cot, weight_first, weight_second = operands
    preact = jnp.dot(rows_in, weight_first, preferred_element_type=jnp.float32)
    hidden = gelu_value(preact).astype(jnp.bfloat16)
    backprop = jnp.dot(rows_cot, weight_second.T, preferred_element_type=jnp.float32)
    grad_pre = (gelu_slope(preact) * backprop).astype(jnp.bfloat16)
    grad_first = jnp.dot(rows_in.T, grad_pre, preferred_element_type=jnp.float32).astype(jnp.bfloat16)
    grad_second = jnp.dot(hidden.T, rows_cot, preferred_element_type=jnp.float32).astype(jnp.bfloat16)
    row_total = rows_in.shape[0]
    split_pre = grad_pre.astype(jnp.float32).reshape(row_total, N_DP, FF // N_DP)
    split_weight = weight_first.astype(jnp.float32).reshape(D, N_DP, FF // N_DP)
    pieces = jnp.einsum("rqf,dqf->qrd", split_pre, split_weight).astype(jnp.bfloat16)
    pieces = lax.optimization_barrier(pieces)
    rows_grad = jnp.sum(pieces.astype(jnp.float32), axis=0).astype(jnp.bfloat16)
    return grad_first, grad_second, rows_grad


def reference(layer_input, output_grad, gate_weights, expert_ids, slot_positions, keep_mask, weight_in, weight_out):
    device_count = TOKENS // TOK_DEV
    slot_total = device_count * EXPERTS * CAP
    source = (jnp.arange(TOKENS, dtype=jnp.int32) // TOK_DEV)[:, None]
    flat_index = (source * (EXPERTS * CAP) + expert_ids * CAP + slot_positions).astype(jnp.int32).reshape(-1)
    keep_float = keep_mask.astype(jnp.float32)[:, :, None]
    spread_input = layer_input.astype(jnp.float32)[:, None, :] * keep_float
    scaled = (gate_weights[:, :, None] * output_grad.astype(jnp.float32)[:, None, :]).astype(jnp.bfloat16)
    scaled = lax.optimization_barrier(scaled)
    spread_cotan = scaled.astype(jnp.float32) * keep_float
    buffer_input = jnp.zeros((slot_total, D), jnp.float32).at[flat_index].add(spread_input.reshape(-1, D)).astype(jnp.bfloat16)
    buffer_cotan = jnp.zeros((slot_total, D), jnp.float32).at[flat_index].add(spread_cotan.reshape(-1, D)).astype(jnp.bfloat16)
    rows_in = buffer_input.reshape(device_count, EXPERTS, CAP, D).transpose(1, 0, 2, 3).reshape(EXPERTS, device_count * CAP, D)
    rows_cot = buffer_cotan.reshape(device_count, EXPERTS, CAP, D).transpose(1, 0, 2, 3).reshape(EXPERTS, device_count * CAP, D)
    grad_first, grad_second, rows_grad = lax.map(expert_backward, (rows_in, rows_cot, weight_in, weight_out))
    back_rows = rows_grad.reshape(EXPERTS, device_count, CAP, D).transpose(1, 0, 2, 3).reshape(slot_total, D)
    picked = back_rows[flat_index].astype(jnp.float32).reshape(TOKENS, 2, D) * keep_float
    input_grad = jnp.sum(picked, axis=1).astype(jnp.bfloat16)
    return (input_grad, grad_first, grad_second)
```

```python
import functools

import jax
import jax.numpy as jnp
from jax import lax
from jax.experimental import pallas as pl
from jax.experimental.pallas import tpu as pltpu
from jax.sharding import PartitionSpec as P

root_coef = 0.7978845608028654
cube_coef = 0.044715
vmem_whole = pl.BlockSpec(memory_space=pltpu.VMEM)
f32 = jnp.float32
bf16 = jnp.bfloat16


def vmem_out(shape, dtype=bf16):
    return pltpu.VMEM(shape, dtype)


def params(mib):
    return pltpu.CompilerParams(vmem_limit_bytes=mib * 1024 * 1024)


def cost(flops, moved, trans=0):
    return pl.CostEstimate(flops=flops, bytes_accessed=moved, transcendentals=trans)


def selector_columns(ids, slots, keep, me, slot_cap, half):
    relative = ids ^ me
    column = (relative & 1) * half + (relative >> 1) * slot_cap + slots
    return jnp.where(keep > 0, column, -1)


def dispatch_kernel(slot_cap, tokens_ref, grads_ref, gate_ref, ids_ref, slots_ref, keep_ref, own_ref, other_ref):
    half = own_ref.shape[0]
    token_count, width = tokens_ref.shape
    me = lax.axis_index("expert")
    column = selector_columns(ids_ref[...], slots_ref[...], keep_ref[...], me, slot_cap, half)
    gate = gate_ref[...]
    for base, out_ref in ((half, other_ref), (0, own_ref)):
        rows = lax.broadcasted_iota(jnp.int32, (half, token_count), 0) + base
        first, second = rows == column[0:1], rows == column[1:2]
        picked = (first | second).astype(f32).astype(bf16)
        scale = jnp.sum(
            jnp.where(first, gate[0:1], 0.0) + jnp.where(second, gate[1:2], 0.0), axis=1, keepdims=True
        )
        out_ref[:, :width] = jnp.dot(picked, tokens_ref[...], preferred_element_type=f32).astype(bf16)
        row_grad = jnp.dot(picked, grads_ref[...], preferred_element_type=f32)
        out_ref[:, width:] = (scale * row_grad).astype(bf16)


def combine_kernel(slot_cap, own_ref, other_ref, ids_ref, slots_ref, keep_ref, out_ref):
    half = own_ref.shape[0]
    token_count = out_ref.shape[0]
    me = lax.axis_index("expert")
    column = selector_columns(ids_ref[...], slots_ref[...], keep_ref[...], me, slot_cap, half)
    total = jnp.zeros(out_ref.shape, f32)
    for base, rows_ref in ((0, own_ref), (half, other_ref)):
        rows = lax.broadcasted_iota(jnp.int32, (half, token_count), 0) + base
        picked = ((rows == column[0:1]) | (rows == column[1:2])).astype(f32).astype(bf16)
        total += lax.dot_general(picked, rows_ref[...], (((0,), (0,)), ((), ())), preferred_element_type=f32)
    out_ref[...] = total.astype(bf16)


def chunk_kernel(n_pieces, tile, *refs):
    pieces = refs[:n_pieces]
    win_ref, wout_ref = refs[n_pieces : n_pieces + 2]
    parts = refs[n_pieces + 2 : 2 * n_pieces + 2]
    rows_ref, hidden_ref, pre_ref, acc_ref = refs[2 * n_pieces + 2 :]
    width = win_ref.shape[0]
    hidden_total = win_ref.shape[1]
    start = 0
    spans = []
    for ref in pieces:
        count = ref.shape[0]
        rows_ref[start : start + count, :] = ref[...]
        spans.append((start, start + count))
        start += count
    for base in range(0, hidden_total, tile):
        cols = slice(base, base + tile)
        preact = jnp.dot(rows_ref[:, :width], win_ref[:, cols], preferred_element_type=f32)
        backprop = lax.dot_general(
            rows_ref[:, width:], wout_ref[cols, :], (((1,), (1,)), ((), ())), preferred_element_type=f32
        )
        square = preact * preact
        tanh_value = jnp.tanh(root_coef * (preact + cube_coef * preact * square))
        one_plus = 0.5 * (1.0 + tanh_value)
        hidden_ref[:, cols] = (preact * one_plus).astype(bf16)
        slope = one_plus + 0.5 * preact * (1.0 - tanh_value * tanh_value) * (
            root_coef + (3.0 * cube_coef * root_coef) * square
        )
        grad_pre = (slope * backprop).astype(bf16)
        pre_ref[:, cols] = grad_pre
        term = lax.dot_general(
            grad_pre, win_ref[:, cols], (((1,), (1,)), ((), ())), preferred_element_type=f32
        )
        if base == 0:
            acc_ref[...] = term
        else:
            acc_ref[...] += term
    for (low, high), ref in zip(spans, parts, strict=True):
        ref[...] = acc_ref[low:high, :].astype(bf16)


def weight_in_kernel(count, width, *refs):
    total = None
    for rows_ref, pre_ref in zip(refs[:count], refs[count : 2 * count], strict=True):
        term = lax.dot_general(
            rows_ref[:, :width], pre_ref[...], (((0,), (0,)), ((), ())), preferred_element_type=f32
        )
        total = term if total is None else total + term
    refs[-1][...] = total.astype(bf16)


def weight_out_kernel(count, width, *refs):
    total = None
    for rows_ref, hidden_ref in zip(refs[:count], refs[count : 2 * count], strict=True):
        term = lax.dot_general(
            hidden_ref[...], rows_ref[:, width:], (((0,), (0,)), ((), ())), preferred_element_type=f32
        )
        total = term if total is None else total + term
    refs[-1][...] = total.astype(bf16)


def swap(value, axis, offset):
    size = lax.axis_size(axis)
    return lax.ppermute(value, axis, [(i, i ^ offset) for i in range(size)])


def body(
    layer_input,
    output_grad,
    gate_weights,
    expert_ids,
    slot_positions,
    keep_mask,
    weight_in,
    weight_out,
):
    token_count, width = layer_input.shape
    owners = lax.axis_size("expert")
    groups = lax.axis_size("dp")
    slot_cap = 3 * token_count // (2 * owners)
    chips = owners // 2
    half = chips * slot_cap
    block = 2 * slot_cap
    gate, ids, slots, keep = gate_weights.T, expert_ids.T, slot_positions.T, keep_mask.T
    win, wout = weight_in[0], weight_out[0]
    hidden_total = win.shape[1]

    own, other = pl.pallas_call(
        functools.partial(dispatch_kernel, slot_cap),
        out_shape=(vmem_out((half, 2 * width)),) * 2,
        in_specs=[vmem_whole] * 6,
        out_specs=(vmem_whole,) * 2,
        compiler_params=params(16),
        name="dispatch",
    )(layer_input, output_grad, gate, ids, slots, keep)
    got = swap(other, "expert", 1)

    arrived = []
    for m in range(chips):
        span = slice(m * slot_cap, (m + 1) * slot_cap)
        rows = jnp.concatenate([own[span], got[span]], axis=0)
        arrived.append(rows if m == 0 else swap(rows, "expert", 2 * m))

    chunk_count = 2
    per_chunk = chips // chunk_count
    chunks = [list(range(c * per_chunk, (c + 1) * per_chunk)) for c in range(chunk_count)]
    returned = [None] * chips
    all_rows, all_hidden, all_pre = [], [], []
    for chunk in chunks:
        mine = jnp.concatenate([arrived[m] for m in chunk], axis=0)
        count = mine.shape[0]
        pieces = [mine] + [swap(mine, "dp", o) for o in range(1, groups)]
        total = groups * count
        outs = pl.pallas_call(
            functools.partial(chunk_kernel, groups, 256),
            out_shape=(vmem_out((count, width)),) * groups
            + (vmem_out((total, 2 * width)), vmem_out((total, hidden_total)), vmem_out((total, hidden_total))),
            in_specs=[vmem_whole] * (groups + 2),
            out_specs=(vmem_whole,) * (groups + 3),
            scratch_shapes=[pltpu.VMEM((total, width), f32)],
            compiler_params=params(32),
            cost_estimate=cost(6 * total * width * hidden_total, 4 * width * hidden_total, total * hidden_total),
            name="chunk",
        )(*pieces, win, wout)
        parts = outs[:groups]
        all_rows.append(outs[groups])
        all_hidden.append(outs[groups + 1])
        all_pre.append(outs[groups + 2])
        summed = parts[0].astype(f32)
        for o in range(1, groups):
            summed = summed + swap(parts[o], "dp", o).astype(f32)
        summed = summed.astype(bf16)
        for i, m in enumerate(chunk):
            piece = summed[i * block : (i + 1) * block]
            returned[m] = piece if m == 0 else swap(piece, "expert", 2 * m)

    weight_call = dict(
        in_specs=[vmem_whole] * (2 * chunk_count),
        out_specs=vmem_whole,
        compiler_params=params(40),
        cost_estimate=cost(2 * block * chips * groups * width * hidden_total, 2 * width * hidden_total),
    )
    grad_in = pl.pallas_call(
        functools.partial(weight_in_kernel, chunk_count, width),
        out_shape=jax.ShapeDtypeStruct((width, hidden_total), bf16),
        name="weight_in_grad",
        **weight_call,
    )(*all_rows, *all_pre)
    grad_out = pl.pallas_call(
        functools.partial(weight_out_kernel, chunk_count, width),
        out_shape=jax.ShapeDtypeStruct((hidden_total, width), bf16),
        name="weight_out_grad",
        **weight_call,
    )(*all_rows, *all_hidden)

    for_partner = jnp.concatenate([r[slot_cap:] for r in returned], axis=0)
    back_other = swap(for_partner, "expert", 1)
    back_own = jnp.concatenate([r[:slot_cap] for r in returned], axis=0)
    input_grad = pl.pallas_call(
        functools.partial(combine_kernel, slot_cap),
        out_shape=jax.ShapeDtypeStruct((token_count, width), bf16),
        in_specs=[vmem_whole] * 5,
        out_specs=vmem_whole,
        compiler_params=params(16),
        name="combine",
    )(back_own, back_other, ids, slots, keep)
    return (input_grad, grad_in[None], grad_out[None])


def solution(mesh):
    tokens = P(("dp", "expert"), None)
    in_specs = (tokens,) * 6 + (P("expert", None, "dp"), P("expert", "dp", None))
    out_specs = (tokens, P("expert", None, "dp"), P("expert", "dp", None))
    return jax.shard_map(body, mesh=mesh, in_specs=in_specs, out_specs=out_specs, check_vma=False)
```

```python
import functools

import jax
import jax.numpy as jnp
from jax import lax
from jax.experimental import pallas as pl
from jax.experimental.pallas import tpu as pltpu
from jax.sharding import PartitionSpec as P

root_coef = 0.7978845608028654
cube_coef = 0.044715
vmem_whole = pl.BlockSpec(memory_space=pltpu.VMEM)
anywhere = pl.BlockSpec(memory_space=pl.ANY)
f32 = jnp.float32
CHUNKS = (((0, 1),), ((2, 3),))
DIRECT = (True, True)
LANES = ((True,), (True,))
AFTER = (0, -1)
TILE = 1280
LOAD = None
GATE = False
bf16 = jnp.bfloat16


def in_hbm(value):
    return pltpu.with_memory_space_constraint(value, pltpu.HBM)


def vmem_out(shape, dtype=bf16):
    return pltpu.VMEM(shape, dtype)


def params(mib):
    return pltpu.CompilerParams(vmem_limit_bytes=mib * 1024 * 1024)


def cost(flops, moved, trans=0):
    return pl.CostEstimate(flops=flops, bytes_accessed=moved, transcendentals=trans)


def selector_columns(ids, slots, keep, me, slot_cap, half):
    relative = ids ^ me
    column = (relative & 1) * half + (relative >> 1) * slot_cap + slots
    return jnp.where(keep > 0, column, -1)


def dispatch_kernel(slot_cap, *refs):
    sources, (own_ref, other_ref), held, sem = refs[:6], refs[6:8], refs[8:14], refs[14]
    copies = [pltpu.make_async_copy(a, b, sem.at[i]) for i, (a, b) in enumerate(zip(sources, held, strict=True))]
    for copy in copies:
        copy.start()
    for copy in copies:
        copy.wait()
    tokens_ref, grads_ref, gate_ref, ids_ref, slots_ref, keep_ref = held
    half = own_ref.shape[0]
    token_count, width = tokens_ref.shape
    me = lax.axis_index("expert")
    column = selector_columns(ids_ref[...], slots_ref[...], keep_ref[...], me, slot_cap, half)
    gate = gate_ref[...]
    for base, out_ref in ((half, other_ref), (0, own_ref)):
        rows = lax.broadcasted_iota(jnp.int32, (half, token_count), 0) + base
        first, second = rows == column[0:1], rows == column[1:2]
        picked = (first | second).astype(f32).astype(bf16)
        scale = jnp.sum(
            jnp.where(first, gate[0:1], 0.0) + jnp.where(second, gate[1:2], 0.0), axis=1, keepdims=True
        )
        out_ref[:, :width] = jnp.dot(picked, tokens_ref[...], preferred_element_type=f32).astype(bf16)
        row_grad = jnp.dot(picked, grads_ref[...], preferred_element_type=f32)
        out_ref[:, width:] = (scale * row_grad).astype(bf16)


def combine_kernel(slot_cap, own_ref, other_ref, ids_ref, slots_ref, keep_ref, out_ref):
    half = own_ref.shape[0]
    token_count = out_ref.shape[0]
    me = lax.axis_index("expert")
    column = selector_columns(ids_ref[...], slots_ref[...], keep_ref[...], me, slot_cap, half)
    total = jnp.zeros(out_ref.shape, f32)
    for base, rows_ref in ((0, own_ref), (half, other_ref)):
        rows = lax.broadcasted_iota(jnp.int32, (half, token_count), 0) + base
        picked = ((rows == column[0:1]) | (rows == column[1:2])).astype(f32).astype(bf16)
        total += lax.dot_general(picked, rows_ref[...], (((0,), (0,)), ((), ())), preferred_element_type=f32)
    out_ref[...] = total.astype(bf16)


def gathered_order(bits):
    order = [0]
    steps = []
    for bit in bits:
        steps.append([o ^ bit for o in order])
        order = order + steps[-1]
    return steps


def scattered_order(bits, groups):
    left = list(range(groups))
    steps = []
    for bit in bits:
        steps.append([o for o in left if o & bit])
        left = [o for o in left if not o & bit]
    return steps


def load_kernel(*refs):
    sources, targets, sem = refs[:2], refs[-3:-1], refs[-1]
    copies = [pltpu.make_async_copy(a, b, sem.at[i]) for i, (a, b) in enumerate(zip(sources, targets, strict=True))]
    for copy in copies:
        copy.start()
    for copy in copies:
        copy.wait()


def chunk_kernel(tile, groups, cuts, places, *refs):
    moved, refs = refs[: len(places)], refs[len(places) :]
    (win_ref, wout_ref), outs = refs[:2], refs[2:]
    sends, kept_ref = outs[:-5], outs[-5]
    rows_ref, hidden_ref, pre_ref, acc_ref = outs[-4:]
    width, hidden_total = win_ref.shape
    count = rows_ref.shape[0] // groups
    for ref, (start, size, low, high, offsets) in zip(moved, places, strict=True):
        for i, o in enumerate(offsets):
            rows_ref[o * count + start : o * count + start + size, low:high] = ref[i * size : (i + 1) * size, :]
    for base in range(0, hidden_total, tile):
        cols = slice(base, base + tile)
        preact = jnp.dot(rows_ref[:, :width], win_ref[:, cols], preferred_element_type=f32)
        backprop = lax.dot_general(
            rows_ref[:, width:], wout_ref[cols, :], (((1,), (1,)), ((), ())), preferred_element_type=f32
        )
        square = preact * preact
        tanh_value = jnp.tanh(root_coef * (preact + cube_coef * preact * square))
        one_plus = 0.5 * (1.0 + tanh_value)
        hidden_ref[:, cols] = (preact * one_plus).astype(bf16)
        slope = one_plus + 0.5 * preact * (1.0 - tanh_value * tanh_value) * (
            root_coef + (3.0 * cube_coef * root_coef) * square
        )
        grad_pre = (slope * backprop).astype(bf16)
        pre_ref[:, cols] = grad_pre
        term = lax.dot_general(
            grad_pre, win_ref[:, cols], (((1,), (1,)), ((), ())), preferred_element_type=f32
        )
        if base == 0:
            acc_ref[...] = term
        else:
            acc_ref[...] += term
    kept_ref[...] = acc_ref[:count, :].astype(bf16)
    for (low, high, offsets), ref in zip(cuts, sends, strict=True):
        for i, o in enumerate(offsets):
            ref[i * (high - low) : (i + 1) * (high - low), :] = acc_ref[o * count + low : o * count + high, :].astype(
                bf16
            )


def stacked(refs, cols):
    return jnp.concatenate([ref[:, cols] for ref in refs], axis=0)


def weight_in_kernel(count, width, *refs):
    rows, pre = stacked(refs[:count], slice(0, width)), stacked(refs[count : 2 * count], slice(None))
    out_ref, done_ref = refs[-2:]
    total = lax.dot_general(rows, pre, (((0,), (0,)), ((), ())), preferred_element_type=f32)
    out_ref[...] = total.astype(bf16)
    done_ref[...] = jnp.zeros(done_ref.shape, bf16)


def weight_out_kernel(count, width, *refs):
    cot = stacked(refs[:count], slice(width, 2 * width))
    hidden = stacked(refs[count : 2 * count], slice(None))
    out_ref, done_ref = refs[-2:]
    total = lax.dot_general(hidden, cot, (((0,), (0,)), ((), ())), preferred_element_type=f32)
    out_ref[...] = total.astype(bf16)
    done_ref[...] = jnp.zeros(done_ref.shape, bf16)


def sum_kernel(*refs):
    total = refs[0][...].astype(f32)
    for ref in refs[1:-2]:
        total = total + ref[...].astype(f32)
    refs[-1][...] = total.astype(bf16)


def pack_kernel(slot_cap, *refs):
    returned, (own_ref, other_ref) = refs[:-3], refs[-2:]
    rows = jnp.concatenate([ref[...].astype(f32) for ref in returned], axis=0)
    rows = rows.reshape(len(returned), 2, slot_cap, rows.shape[-1])
    for part, ref in ((0, own_ref), (1, other_ref)):
        ref[...] = rows[:, part].reshape(ref.shape).astype(bf16)


def added(value, offsets, received, size):
    total = value.astype(f32)
    for held, part in received:
        at = [held.index(o) * size for o in offsets]
        total = total + jnp.concatenate([part[i : i + size] for i in at], axis=0).astype(f32)
    return total.astype(bf16)


def swap(value, axis, offset):
    size = lax.axis_size(axis)
    return lax.ppermute(value, axis, [(i, i ^ offset) for i in range(size)])


def body(
    layer_input,
    output_grad,
    gate_weights,
    expert_ids,
    slot_positions,
    keep_mask,
    weight_in,
    weight_out,
):
    token_count, width = layer_input.shape
    owners = lax.axis_size("expert")
    groups = lax.axis_size("dp")
    slot_cap = 3 * token_count // (2 * owners)
    chips = owners // 2
    half = chips * slot_cap
    block = 2 * slot_cap
    gate, ids, slots, keep = gate_weights.T, expert_ids.T, slot_positions.T, keep_mask.T
    win, wout = weight_in[0], weight_out[0]
    hidden_total = win.shape[1]

    arguments = (layer_input, output_grad, gate, ids, slots, keep)
    own, other = pl.pallas_call(
        functools.partial(dispatch_kernel, slot_cap),
        out_shape=(vmem_out((half, 2 * width)),) * 2,
        in_specs=[pl.BlockSpec(memory_space=pltpu.HBM)] * 6,
        out_specs=(vmem_whole,) * 2,
        scratch_shapes=[pltpu.VMEM(a.shape, a.dtype) for a in arguments] + [pltpu.SemaphoreType.DMA((6,))],
        compiler_params=params(16),
        name="dispatch",
    )(*[in_hbm(a) for a in arguments])
    got = swap(other, "expert", 1)

    arrived = []
    for m in range(chips):
        span = slice(m * slot_cap, (m + 1) * slot_cap)
        rows = jnp.concatenate([own[span], got[span]], axis=0)
        arrived.append(rows if m == 0 else swap(rows, "expert", 2 * m))

    quarter = chips // 4
    chunks = [[[q * quarter + i for q in quarters for i in range(quarter)] for quarters in c] for c in CHUNKS]
    chunk_count = len(chunks)
    returned = [None] * chips
    all_rows, all_hidden, all_pre = [], [], []
    bits = [1 << i for i in range(groups.bit_length() - 1)]
    lanes = (bits, bits[::-1])
    steps = len(bits)
    weights = pl.pallas_call(
        load_kernel,
        out_shape=(vmem_out(win.shape), vmem_out(wout.shape)),
        in_specs=[pl.BlockSpec(memory_space=pltpu.HBM)] * 2 + [anywhere],
        out_specs=(vmem_whole,) * 2,
        scratch_shapes=[pltpu.SemaphoreType.DMA((2,))],
        compiler_params=params(16),
        cost_estimate=cost(0, 8 * width * hidden_total),
        name="load",
    )(in_hbm(win), in_hbm(wout), got if LOAD is None else arrived[LOAD * quarter])
    sums_of = []
    all_count = block * chips * groups
    weight_call = dict(
        in_specs=[vmem_whole] * (2 * chunk_count) + [anywhere],
        out_specs=(vmem_whole,) * 2,
        compiler_params=params(40),
        cost_estimate=cost(2 * all_count * width * hidden_total, 2 * width * hidden_total),
    )

    def weight_in_call(after):
        return pl.pallas_call(
            functools.partial(weight_in_kernel, chunk_count, width),
            out_shape=(jax.ShapeDtypeStruct((width, hidden_total), bf16), vmem_out((16, 128))),
            name="weight_in_grad",
            **weight_call,
        )(*all_rows, *all_pre, after)

    def weight_out_call(after):
        return pl.pallas_call(
            functools.partial(weight_out_kernel, chunk_count, width),
            out_shape=(jax.ShapeDtypeStruct((hidden_total, width), bf16), vmem_out((16, 128))),
            name="weight_out_grad",
            **weight_call,
        )(*all_rows, *all_hidden, after)

    for number, chunk in enumerate(chunks):
        moved, places, start = [], [], 0
        for by_lanes, group in zip(LANES[number], chunk, strict=True):
            mine = jnp.concatenate([arrived[m] for m in group], axis=0)
            size = mine.shape[0]
            if by_lanes:
                for lane in range(2):
                    held, low = [mine[:, lane * width : (lane + 1) * width]], lane * width
                    orders = [[0]] + gathered_order(lanes[lane])
                    for step in range(steps):
                        held.append(swap(jnp.concatenate(held, axis=0), "dp", lanes[lane][step]))
                    moved += held
                    places += [(start, size, low, low + width, offsets) for offsets in orders]
            else:
                for o in range(groups):
                    moved.append(swap(mine, "dp", o) if o else mine)
                    places.append((start, size, 0, 2 * width, [o]))
            start += size
        inside = [m for group in chunk for m in group]
        count = len(inside) * block
        total = groups * count
        cut = count // 32 * 16
        if DIRECT[number]:
            cuts = [(0, count, [o]) for o in range(1, groups)]
        else:
            cuts = [
                (low, high, offsets)
                for lane, (low, high) in zip(lanes, ((0, cut), (cut, count)), strict=True)
                for offsets in scattered_order(lane, groups)
            ]
        outs = pl.pallas_call(
            functools.partial(chunk_kernel, TILE, groups, cuts, places),
            out_shape=tuple(vmem_out((len(offsets) * (high - low), width)) for low, high, offsets in cuts)
            + (
                vmem_out((count, width)),
                vmem_out((total, 2 * width)),
                vmem_out((total, hidden_total)),
                vmem_out((total, hidden_total)),
            ),
            in_specs=[vmem_whole] * (len(moved) + 2),
            out_specs=(vmem_whole,) * (len(cuts) + 4),
            scratch_shapes=[pltpu.VMEM((total, width), f32)],
            compiler_params=params(32),
            cost_estimate=cost(6 * total * width * hidden_total, 4 * width * hidden_total, total * hidden_total),
            name="chunk",
        )(*moved, *weights)
        sends, (kept, rows_all, hidden, pre) = outs[:-4], outs[-4:]
        all_rows.append(rows_all)
        all_hidden.append(hidden)
        all_pre.append(pre)
        if DIRECT[number]:
            terms = [kept] + [swap(v, "dp", offsets[0]) for (_, _, offsets), v in zip(cuts, sends, strict=True)]
            if number == len(chunks) - 1:
                grad_in, done = weight_in_call(sums_of[0])
                summed = pl.pallas_call(
                    sum_kernel,
                    out_shape=vmem_out((count, width)),
                    in_specs=[vmem_whole] * groups + [anywhere],
                    out_specs=vmem_whole,
                    compiler_params=params(16),
                    name="sum",
                )(*terms, done)
            else:
                summed = sum(t.astype(f32) for t in terms).astype(bf16)
        else:
            finals = []
            for lane, bits_of in enumerate(lanes):
                low, high = (0, cut) if lane == 0 else (cut, count)
                received = []
                for step in range(steps):
                    value, offsets = sends[lane * steps + step], cuts[lane * steps + step][2]
                    if received:
                        value = added(value, offsets, received, high - low)
                    received.append(([o ^ bits_of[step] for o in offsets], swap(value, "dp", bits_of[step])))
                finals.append(added(kept[low:high], [0], received, high - low))
            summed = jnp.concatenate(finals, axis=0)
        sums_of.append(summed)
        for i, m in enumerate(inside):
            piece = summed[i * block : (i + 1) * block]
            returned[m] = piece if m == 0 else swap(piece, "expert", 2 * m)

    grad_out, done = weight_out_call(sums_of[-1])
    back_own, for_partner = pl.pallas_call(
        functools.partial(pack_kernel, slot_cap),
        out_shape=(vmem_out((half, width)),) * 2,
        in_specs=[vmem_whole] * chips + [anywhere],
        out_specs=(vmem_whole,) * 2,
        compiler_params=params(16),
        name="pack",
    )(*returned, done)
    back_other = swap(for_partner, "expert", 1)
    input_grad = pl.pallas_call(
        functools.partial(combine_kernel, slot_cap),
        out_shape=jax.ShapeDtypeStruct((token_count, width), bf16),
        in_specs=[vmem_whole] * 5,
        out_specs=vmem_whole,
        compiler_params=params(16),
        name="combine",
    )(back_own, back_other, ids, slots, keep)
    return (input_grad, grad_in[None], grad_out[None])


def solution(mesh):
    tokens = P(("dp", "expert"), None)
    in_specs = (tokens,) * 6 + (P("expert", None, "dp"), P("expert", "dp", None))
    out_specs = (tokens, P("expert", None, "dp"), P("expert", "dp", None))
    return jax.shard_map(body, mesh=mesh, in_specs=in_specs, out_specs=out_specs, check_vma=False)
```

```python
import functools

import jax
import jax.numpy as jnp
from jax import lax
from jax.experimental import pallas as pl
from jax.experimental.pallas import tpu as pltpu
from jax.sharding import PartitionSpec as P

root_coef = 0.7978845608028654
cube_coef = 0.044715
vmem_whole = pl.BlockSpec(memory_space=pltpu.VMEM)
anywhere = pl.BlockSpec(memory_space=pl.ANY)
f32 = jnp.float32
CHUNKS = (((0,), (1,)), ((2,), (3,)))
DIRECT = (False, True)
TILE = 1280
C_CHUNK = 1.0
C_LOAD = 1.0
C_W = 1.0
LOAD = None
WAIT_Z = False
DEFER = 1
HOLD = False
EARLY_LOAD = False
FIRST_LOAD = True
HOLD2 = 0
Z3 = False
bf16 = jnp.bfloat16


def in_hbm(value):
    return pltpu.with_memory_space_constraint(value, pltpu.HBM)


def vmem_out(shape, dtype=bf16):
    return pltpu.VMEM(shape, dtype)


def params(mib):
    return pltpu.CompilerParams(vmem_limit_bytes=mib * 1024 * 1024)


def cost(flops, moved, trans=0):
    return pl.CostEstimate(flops=flops, bytes_accessed=moved, transcendentals=trans)


def selector_columns(ids, slots, keep, me, slot_cap, half):
    relative = ids ^ me
    column = (relative & 1) * half + (relative >> 1) * slot_cap + slots
    return jnp.where(keep > 0, column, -1)


def dispatch_kernel(slot_cap, *refs):
    sources, (own_ref, other_ref), held, sem = refs[:6], refs[6:8], refs[8:14], refs[14]
    copies = [pltpu.make_async_copy(a, b, sem.at[i]) for i, (a, b) in enumerate(zip(sources, held, strict=True))]
    for copy in copies:
        copy.start()
    for copy in copies:
        copy.wait()
    tokens_ref, grads_ref, gate_ref, ids_ref, slots_ref, keep_ref = held
    half = own_ref.shape[0]
    token_count, width = tokens_ref.shape
    me = lax.axis_index("expert")
    column = selector_columns(ids_ref[...], slots_ref[...], keep_ref[...], me, slot_cap, half)
    gate = gate_ref[...]
    for base, out_ref in ((half, other_ref), (0, own_ref)):
        rows = lax.broadcasted_iota(jnp.int32, (half, token_count), 0) + base
        first, second = rows == column[0:1], rows == column[1:2]
        picked = (first | second).astype(f32).astype(bf16)
        scale = jnp.sum(
            jnp.where(first, gate[0:1], 0.0) + jnp.where(second, gate[1:2], 0.0), axis=1, keepdims=True
        )
        out_ref[:, :width] = jnp.dot(picked, tokens_ref[...], preferred_element_type=f32).astype(bf16)
        row_grad = jnp.dot(picked, grads_ref[...], preferred_element_type=f32)
        out_ref[:, width:] = (scale * row_grad).astype(bf16)


def combine_kernel(slot_cap, own_ref, other_ref, ids_ref, slots_ref, keep_ref, out_ref):
    half = own_ref.shape[0]
    token_count = out_ref.shape[0]
    me = lax.axis_index("expert")
    column = selector_columns(ids_ref[...], slots_ref[...], keep_ref[...], me, slot_cap, half)
    total = jnp.zeros(out_ref.shape, f32)
    for base, rows_ref in ((0, own_ref), (half, other_ref)):
        rows = lax.broadcasted_iota(jnp.int32, (half, token_count), 0) + base
        picked = ((rows == column[0:1]) | (rows == column[1:2])).astype(f32).astype(bf16)
        total += lax.dot_general(picked, rows_ref[...], (((0,), (0,)), ((), ())), preferred_element_type=f32)
    out_ref[...] = total.astype(bf16)


def load_kernel(*refs):
    sources, targets, sem = refs[:2], refs[-3:-1], refs[-1]
    copies = [pltpu.make_async_copy(a, b, sem.at[i]) for i, (a, b) in enumerate(zip(sources, targets, strict=True))]
    for copy in copies:
        copy.start()
    for copy in copies:
        copy.wait()


def chunk_kernel(tile, groups, levels, places, *refs):
    moved, refs = refs[: len(places)], refs[len(places) :]
    (win_ref, wout_ref), outs = refs[:2], refs[2:]
    sends, kept_ref = outs[:-5], outs[-5]
    rows_ref, hidden_ref, pre_ref, acc_ref = outs[-4:]
    width, hidden_total = win_ref.shape
    count = rows_ref.shape[0] // groups
    for ref, (start, size, first) in zip(moved, places, strict=True):
        for i in range(ref.shape[0] // size):
            at = (first + i) * count + start
            rows_ref[at : at + size, :] = ref[i * size : (i + 1) * size, :]
    for base in range(0, hidden_total, tile):
        cols = slice(base, base + tile)
        preact = jnp.dot(rows_ref[:, :width], win_ref[:, cols], preferred_element_type=f32)
        backprop = lax.dot_general(
            rows_ref[:, width:], wout_ref[cols, :], (((1,), (1,)), ((), ())), preferred_element_type=f32
        )
        square = preact * preact
        tanh_value = jnp.tanh(root_coef * (preact + cube_coef * preact * square))
        one_plus = 0.5 * (1.0 + tanh_value)
        hidden_ref[:, cols] = (preact * one_plus).astype(bf16)
        slope = one_plus + 0.5 * preact * (1.0 - tanh_value * tanh_value) * (
            root_coef + (3.0 * cube_coef * root_coef) * square
        )
        grad_pre = (slope * backprop).astype(bf16)
        pre_ref[:, cols] = grad_pre
        term = lax.dot_general(
            grad_pre, win_ref[:, cols], (((1,), (1,)), ((), ())), preferred_element_type=f32
        )
        if base == 0:
            acc_ref[...] = term
        else:
            acc_ref[...] += term
    kept_ref[...] = acc_ref[:count, :].astype(bf16)
    for (low, high), ref in zip(levels, sends, strict=True):
        ref[...] = acc_ref[low * count : high * count, :].astype(bf16)


def stacked(refs, cols):
    return jnp.concatenate([ref[:, cols] for ref in refs], axis=0)


def weight_in_kernel(count, width, *refs):
    rows, pre = stacked(refs[:count], slice(0, width)), stacked(refs[count : 2 * count], slice(None))
    out_ref, done_ref = refs[-2:]
    total = lax.dot_general(rows, pre, (((0,), (0,)), ((), ())), preferred_element_type=f32)
    out_ref[...] = total.astype(bf16)
    done_ref[...] = jnp.zeros(done_ref.shape, bf16)


def weight_out_kernel(count, width, *refs):
    cot = stacked(refs[:count], slice(width, 2 * width))
    hidden = stacked(refs[count : 2 * count], slice(None))
    out_ref, done_ref = refs[-2:]
    total = lax.dot_general(hidden, cot, (((0,), (0,)), ((), ())), preferred_element_type=f32)
    out_ref[...] = total.astype(bf16)
    done_ref[...] = jnp.zeros(done_ref.shape, bf16)


def join_kernel(count, *refs):
    start = 0
    for ref in refs[:count]:
        refs[-1][start : start + ref.shape[0], :] = ref[...]
        start += ref.shape[0]


def join(values, after):
    rows = sum(v.shape[0] for v in values)
    return pl.pallas_call(
        functools.partial(join_kernel, len(values)),
        out_shape=vmem_out((rows, values[0].shape[1])),
        in_specs=[vmem_whole] * len(values) + [anywhere] * len(after),
        out_specs=vmem_whole,
        compiler_params=params(16),
        name="join",
    )(*values, *after)


def add_rows(values, after):
    return pl.pallas_call(
        sum_kernel,
        out_shape=vmem_out(values[0].shape),
        in_specs=[vmem_whole] * len(values) + [anywhere],
        out_specs=vmem_whole,
        compiler_params=params(16),
        name="sum",
    )(*values, after)


def sum_kernel(*refs):
    total = refs[0][...].astype(f32)
    for ref in refs[1:-2]:
        total = total + ref[...].astype(f32)
    refs[-1][...] = total.astype(bf16)


def pack_kernel(slot_cap, *refs):
    returned, (own_ref, other_ref) = refs[:-3], refs[-2:]
    rows = jnp.concatenate([ref[...].astype(f32) for ref in returned], axis=0)
    rows = rows.reshape(len(returned), 2, slot_cap, rows.shape[-1])
    for part, ref in ((0, own_ref), (1, other_ref)):
        ref[...] = rows[:, part].reshape(ref.shape).astype(bf16)


def swap(value, axis, offset):
    size = lax.axis_size(axis)
    return lax.ppermute(value, axis, [(i, i ^ offset) for i in range(size)])


def swap_groups(value, position):
    groups, owners = lax.axis_size("dp"), lax.axis_size("expert")
    bits = [1 << i for i in range(groups.bit_length() - 1)]
    offsets = [sum(b for i, b in enumerate(order) if position >> i & 1) for order in (bits, bits[::-1])]
    pairs = [(d * owners + e, (d ^ offsets[e & 1]) * owners + e) for d in range(groups) for e in range(owners)]
    return lax.ppermute(value, ("dp", "expert"), pairs)


def body(
    layer_input,
    output_grad,
    gate_weights,
    expert_ids,
    slot_positions,
    keep_mask,
    weight_in,
    weight_out,
):
    token_count, width = layer_input.shape
    owners = lax.axis_size("expert")
    groups = lax.axis_size("dp")
    slot_cap = 3 * token_count // (2 * owners)
    chips = owners // 2
    half = chips * slot_cap
    block = 2 * slot_cap
    gate, ids, slots, keep = gate_weights.T, expert_ids.T, slot_positions.T, keep_mask.T
    win, wout = weight_in[0], weight_out[0]
    hidden_total = win.shape[1]

    arguments = (layer_input, output_grad, gate, ids, slots, keep)
    own, other = pl.pallas_call(
        functools.partial(dispatch_kernel, slot_cap),
        out_shape=(vmem_out((half, 2 * width)),) * 2,
        in_specs=[pl.BlockSpec(memory_space=pltpu.HBM)] * 6,
        out_specs=(vmem_whole,) * 2,
        scratch_shapes=[pltpu.VMEM(a.shape, a.dtype) for a in arguments] + [pltpu.SemaphoreType.DMA((6,))],
        compiler_params=params(16),
        name="dispatch",
    )(*[in_hbm(a) for a in arguments])
    got = swap(other, "expert", 1)

    arrived = []
    for m in range(chips):
        span = slice(m * slot_cap, (m + 1) * slot_cap)
        rows = jnp.concatenate([own[span], got[span]], axis=0)
        if Z3 and m == chips - 1:
            rows = join([rows], [arrived[1]])
        arrived.append(rows if m == 0 else swap(rows, "expert", 2 * m))

    quarter = chips // 4
    chunks = [[[q * quarter + i for q in quarters for i in range(quarter)] for quarters in c] for c in CHUNKS]
    chunk_count = len(chunks)
    returned = [None] * chips
    all_rows, all_hidden, all_pre = [], [], []
    steps = groups.bit_length() - 1
    weights = pl.pallas_call(
        load_kernel,
        out_shape=(vmem_out(win.shape), vmem_out(wout.shape)),
        in_specs=[pl.BlockSpec(memory_space=pltpu.HBM)] * 2 + [anywhere],
        out_specs=(vmem_whole,) * 2,
        scratch_shapes=[pltpu.SemaphoreType.DMA((2,))],
        compiler_params=params(16),
        cost_estimate=cost(0, int(C_LOAD * 8 * width * hidden_total)),
        name="load",
    )(in_hbm(win), in_hbm(wout), got if LOAD is None else arrived[LOAD * quarter])
    sums_of = []
    all_count = block * chips * groups
    weight_call = dict(
        in_specs=[vmem_whole] * (2 * chunk_count) + [anywhere],
        out_specs=(vmem_whole,) * 2,
        compiler_params=params(40),
        cost_estimate=cost(int(C_W * 2 * all_count * width * hidden_total), int(C_W * 2 * width * hidden_total)),
    )

    def weight_in_call(after):
        return pl.pallas_call(
            functools.partial(weight_in_kernel, chunk_count, width),
            out_shape=(jax.ShapeDtypeStruct((width, hidden_total), bf16), vmem_out((16, 128))),
            name="weight_in_grad",
            **weight_call,
        )(*all_rows, *all_pre, after)

    def weight_out_call(after):
        return pl.pallas_call(
            functools.partial(weight_out_kernel, chunk_count, width),
            out_shape=(jax.ShapeDtypeStruct((hidden_total, width), bf16), vmem_out((16, 128))),
            name="weight_out_grad",
            **weight_call,
        )(*all_rows, *all_hidden, after)

    deferred = []
    for number, chunk in enumerate(chunks):
        moved, places, start = [], [], 0
        for group in chunk:
            held = [jnp.concatenate([arrived[m] for m in group], axis=0)]
            size = held[0].shape[0]
            if HOLD and number:
                held = [join(held, early)]
            if EARLY_LOAD and not number and group is chunk[-1]:
                held = [join(held, weights[:1])]
            if FIRST_LOAD and not number and group is chunk[0]:
                held = [join(held, weights[:1])]
            if HOLD2 and number:
                held = [join(held, first[1 : HOLD2 + 1])]
            for step in range(steps):
                after = [arrived[m] for group in chunks[-1] for m in group] if WAIT_Z and not number and step else []
                both = join(held, after) if after else jnp.concatenate(held, axis=0)
                held.append(swap_groups(both, 1 << step))
            early = [held[1]]
            if not number and group is chunk[0]:
                first = held
            moved += held
            places += [(start, size, 0)] + [(start, size, 1 << step) for step in range(steps)]
            start += size
        inside = [m for group in chunk for m in group]
        count = len(inside) * block
        total = groups * count
        if DIRECT[number]:
            levels = [(p, p + 1) for p in range(1, groups)]
        else:
            levels = [(1 << step, 2 << step) for step in reversed(range(steps))]
        outs = pl.pallas_call(
            functools.partial(chunk_kernel, TILE, groups, levels, places),
            out_shape=tuple(vmem_out(((high - low) * count, width)) for low, high in levels)
            + (
                vmem_out((count, width)),
                vmem_out((total, 2 * width)),
                vmem_out((total, hidden_total)),
                vmem_out((total, hidden_total)),
            ),
            in_specs=[vmem_whole] * (len(moved) + 2),
            out_specs=(vmem_whole,) * (len(levels) + 4),
            scratch_shapes=[pltpu.VMEM((total, width), f32)],
            compiler_params=params(32),
            cost_estimate=cost(int(C_CHUNK * 6 * total * width * hidden_total), int(C_CHUNK * 4 * width * hidden_total), int(C_CHUNK * total * hidden_total)),
            name="chunk",
        )(*moved, *weights)
        sends, (kept, rows_all, hidden, pre) = outs[:-4], outs[-4:]
        all_rows.append(rows_all)
        all_hidden.append(hidden)
        all_pre.append(pre)
        deferred.append((inside, count, levels, sends, kept))

    def reduced(number, after):
        inside, count, levels, sends, kept = deferred[number]
        terms = [kept]
        if DIRECT[number]:
            terms += [swap_groups(value, p) for (p, _), value in zip(levels, sends, strict=True)]
        else:
            parts = []
            for (low, high), value in zip(levels, sends, strict=True):
                if parts:
                    value = add_rows([value] + [part[low * count : high * count] for part in parts], after[0])
                elif DEFER > 1:
                    value = join([value], after)
                parts.append(swap_groups(value, low))
            terms += [part if part.shape[0] == count else part[:count] for part in parts]
        return terms

    last = len(chunks) - 1
    for number in range(last):
        terms = reduced(number, [deferred[last if DEFER else number][-1]])
        sums_of.append(sum(t.astype(f32) for t in terms).astype(bf16))
    terms = reduced(last, [deferred[last][-1]])
    grad_in, done = weight_in_call(sums_of[0])
    sums_of.append(add_rows(terms, done))
    for (inside, *_), summed in zip(deferred, sums_of, strict=True):
        for i, m in enumerate(inside):
            piece = summed[i * block : (i + 1) * block]
            returned[m] = piece if m == 0 else swap(piece, "expert", 2 * m)

    grad_out, done = weight_out_call(sums_of[-1])
    back_own, for_partner = pl.pallas_call(
        functools.partial(pack_kernel, slot_cap),
        out_shape=(vmem_out((half, width)),) * 2,
        in_specs=[vmem_whole] * chips + [anywhere],
        out_specs=(vmem_whole,) * 2,
        compiler_params=params(16),
        name="pack",
    )(*returned, done)
    back_other = swap(for_partner, "expert", 1)
    input_grad = pl.pallas_call(
        functools.partial(combine_kernel, slot_cap),
        out_shape=jax.ShapeDtypeStruct((token_count, width), bf16),
        in_specs=[vmem_whole] * 5,
        out_specs=vmem_whole,
        compiler_params=params(16),
        name="combine",
    )(back_own, back_other, ids, slots, keep)
    return (input_grad, grad_in[None], grad_out[None])


def solution(mesh):
    tokens = P(("dp", "expert"), None)
    in_specs = (tokens,) * 6 + (P("expert", None, "dp"), P("expert", "dp", None))
    out_specs = (tokens, P("expert", None, "dp"), P("expert", "dp", None))
    return jax.shard_map(body, mesh=mesh, in_specs=in_specs, out_specs=out_specs, check_vma=False)
```

```python
import functools

import jax
import jax.numpy as jnp
from jax import lax
from jax.experimental import pallas as pl
from jax.experimental.pallas import tpu as pltpu
from jax.sharding import PartitionSpec as P

root_coef = 0.7978845608028654
cube_coef = 0.044715
vmem_whole = pl.BlockSpec(memory_space=pltpu.VMEM)
anywhere = pl.BlockSpec(memory_space=pl.ANY)
f32 = jnp.float32
CHUNKS = (((0,), (1,)), ((2,), (3,)))
DIRECT = (False, True)
TILE = 1280
C_CHUNK = 1.0
C_LOAD = 1.0
C_W = 1.0
LOAD = None
WAIT_Z = False
DEFER = 3
HOLD = False
EARLY_LOAD = False
Z1LAST = False
W_AFTER = -1
IN_TURN = True
FIRST_SEND = True
FIRST_LOAD = True
HOLD2 = 0
Z3 = False
bf16 = jnp.bfloat16


def in_hbm(value):
    return pltpu.with_memory_space_constraint(value, pltpu.HBM)


def vmem_out(shape, dtype=bf16):
    return pltpu.VMEM(shape, dtype)


def params(mib):
    return pltpu.CompilerParams(vmem_limit_bytes=mib * 1024 * 1024)


def cost(flops, moved, trans=0):
    return pl.CostEstimate(flops=flops, bytes_accessed=moved, transcendentals=trans)


def selector_columns(ids, slots, keep, me, slot_cap, half):
    relative = ids ^ me
    column = (relative & 1) * half + (relative >> 1) * slot_cap + slots
    return jnp.where(keep > 0, column, -1)


def dispatch_kernel(slot_cap, *refs):
    sources, (own_ref, other_ref), held, sem = refs[:6], refs[6:8], refs[8:14], refs[14]
    copies = [pltpu.make_async_copy(a, b, sem.at[i]) for i, (a, b) in enumerate(zip(sources, held, strict=True))]
    for copy in copies:
        copy.start()
    for copy in copies:
        copy.wait()
    tokens_ref, grads_ref, gate_ref, ids_ref, slots_ref, keep_ref = held
    half = own_ref.shape[0]
    token_count, width = tokens_ref.shape
    me = lax.axis_index("expert")
    column = selector_columns(ids_ref[...], slots_ref[...], keep_ref[...], me, slot_cap, half)
    gate = gate_ref[...]
    for base, out_ref in ((half, other_ref), (0, own_ref)):
        rows = lax.broadcasted_iota(jnp.int32, (half, token_count), 0) + base
        first, second = rows == column[0:1], rows == column[1:2]
        picked = (first | second).astype(f32).astype(bf16)
        scale = jnp.sum(
            jnp.where(first, gate[0:1], 0.0) + jnp.where(second, gate[1:2], 0.0), axis=1, keepdims=True
        )
        out_ref[:, :width] = jnp.dot(picked, tokens_ref[...], preferred_element_type=f32).astype(bf16)
        row_grad = jnp.dot(picked, grads_ref[...], preferred_element_type=f32)
        out_ref[:, width:] = (scale * row_grad).astype(bf16)


def combine_kernel(slot_cap, own_ref, other_ref, ids_ref, slots_ref, keep_ref, out_ref):
    half = own_ref.shape[0]
    token_count = out_ref.shape[0]
    me = lax.axis_index("expert")
    column = selector_columns(ids_ref[...], slots_ref[...], keep_ref[...], me, slot_cap, half)
    total = jnp.zeros(out_ref.shape, f32)
    for base, rows_ref in ((0, own_ref), (half, other_ref)):
        rows = lax.broadcasted_iota(jnp.int32, (half, token_count), 0) + base
        picked = ((rows == column[0:1]) | (rows == column[1:2])).astype(f32).astype(bf16)
        total += lax.dot_general(picked, rows_ref[...], (((0,), (0,)), ((), ())), preferred_element_type=f32)
    out_ref[...] = total.astype(bf16)


def load_kernel(*refs):
    sources, targets, sem = refs[:2], refs[-3:-1], refs[-1]
    copies = [pltpu.make_async_copy(a, b, sem.at[i]) for i, (a, b) in enumerate(zip(sources, targets, strict=True))]
    for copy in copies:
        copy.start()
    for copy in copies:
        copy.wait()


def chunk_kernel(tile, groups, levels, places, *refs):
    moved, refs = refs[: len(places)], refs[len(places) :]
    (win_ref, wout_ref), outs = refs[:2], refs[3:]
    sends, kept_ref = outs[:-5], outs[-5]
    rows_ref, hidden_ref, pre_ref, acc_ref = outs[-4:]
    width, hidden_total = win_ref.shape
    count = rows_ref.shape[0] // groups
    for ref, (start, size, first) in zip(moved, places, strict=True):
        for i in range(ref.shape[0] // size):
            at = (first + i) * count + start
            rows_ref[at : at + size, :] = ref[i * size : (i + 1) * size, :]
    for base in range(0, hidden_total, tile):
        cols = slice(base, base + tile)
        preact = jnp.dot(rows_ref[:, :width], win_ref[:, cols], preferred_element_type=f32)
        backprop = lax.dot_general(
            rows_ref[:, width:], wout_ref[cols, :], (((1,), (1,)), ((), ())), preferred_element_type=f32
        )
        square = preact * preact
        tanh_value = jnp.tanh(root_coef * (preact + cube_coef * preact * square))
        one_plus = 0.5 * (1.0 + tanh_value)
        hidden_ref[:, cols] = (preact * one_plus).astype(bf16)
        slope = one_plus + 0.5 * preact * (1.0 - tanh_value * tanh_value) * (
            root_coef + (3.0 * cube_coef * root_coef) * square
        )
        grad_pre = (slope * backprop).astype(bf16)
        pre_ref[:, cols] = grad_pre
        term = lax.dot_general(
            grad_pre, win_ref[:, cols], (((1,), (1,)), ((), ())), preferred_element_type=f32
        )
        if base == 0:
            acc_ref[...] = term
        else:
            acc_ref[...] += term
    kept_ref[...] = acc_ref[:count, :].astype(bf16)
    for (low, high), ref in zip(levels, sends, strict=True):
        ref[...] = acc_ref[low * count : high * count, :].astype(bf16)


def stacked(refs, cols):
    return jnp.concatenate([ref[:, cols] for ref in refs], axis=0)


def weight_in_kernel(count, width, *refs):
    rows, pre = stacked(refs[:count], slice(0, width)), stacked(refs[count : 2 * count], slice(None))
    out_ref, done_ref = refs[-2:]
    total = lax.dot_general(rows, pre, (((0,), (0,)), ((), ())), preferred_element_type=f32)
    out_ref[...] = total.astype(bf16)
    done_ref[...] = jnp.zeros(done_ref.shape, bf16)


def weight_out_kernel(count, width, *refs):
    cot = stacked(refs[:count], slice(width, 2 * width))
    hidden = stacked(refs[count : 2 * count], slice(None))
    out_ref, done_ref = refs[-2:]
    total = lax.dot_general(hidden, cot, (((0,), (0,)), ((), ())), preferred_element_type=f32)
    out_ref[...] = total.astype(bf16)
    done_ref[...] = jnp.zeros(done_ref.shape, bf16)


def join_kernel(count, *refs):
    start = 0
    for ref in refs[:count]:
        refs[-1][start : start + ref.shape[0], :] = ref[...]
        start += ref.shape[0]


def join(values, after):
    rows = sum(v.shape[0] for v in values)
    return pl.pallas_call(
        functools.partial(join_kernel, len(values)),
        out_shape=vmem_out((rows, values[0].shape[1])),
        in_specs=[vmem_whole] * len(values) + [anywhere] * len(after),
        out_specs=vmem_whole,
        compiler_params=params(16),
        name="join",
    )(*values, *after)


def add_rows(values, after):
    return pl.pallas_call(
        sum_kernel,
        out_shape=vmem_out(values[0].shape),
        in_specs=[vmem_whole] * len(values) + [anywhere],
        out_specs=vmem_whole,
        compiler_params=params(16),
        name="sum",
    )(*values, after)


def sum_kernel(*refs):
    total = refs[0][...].astype(f32)
    for ref in refs[1:-2]:
        total = total + ref[...].astype(f32)
    refs[-1][...] = total.astype(bf16)


def pack_kernel(slot_cap, *refs):
    returned, (own_ref, other_ref) = refs[:-3], refs[-2:]
    rows = jnp.concatenate([ref[...].astype(f32) for ref in returned], axis=0)
    rows = rows.reshape(len(returned), 2, slot_cap, rows.shape[-1])
    for part, ref in ((0, own_ref), (1, other_ref)):
        ref[...] = rows[:, part].reshape(ref.shape).astype(bf16)


def swap(value, axis, offset):
    size = lax.axis_size(axis)
    return lax.ppermute(value, axis, [(i, i ^ offset) for i in range(size)])


def swap_groups(value, position):
    groups, owners = lax.axis_size("dp"), lax.axis_size("expert")
    bits = [1 << i for i in range(groups.bit_length() - 1)]
    offsets = [sum(b for i, b in enumerate(order) if position >> i & 1) for order in (bits, bits[::-1])]
    pairs = [(d * owners + e, (d ^ offsets[e & 1]) * owners + e) for d in range(groups) for e in range(owners)]
    return lax.ppermute(value, ("dp", "expert"), pairs)


def body(
    layer_input,
    output_grad,
    gate_weights,
    expert_ids,
    slot_positions,
    keep_mask,
    weight_in,
    weight_out,
):
    token_count, width = layer_input.shape
    owners = lax.axis_size("expert")
    groups = lax.axis_size("dp")
    slot_cap = 3 * token_count // (2 * owners)
    chips = owners // 2
    half = chips * slot_cap
    block = 2 * slot_cap
    gate, ids, slots, keep = gate_weights.T, expert_ids.T, slot_positions.T, keep_mask.T
    win, wout = weight_in[0], weight_out[0]
    hidden_total = win.shape[1]

    arguments = (layer_input, output_grad, gate, ids, slots, keep)
    own, other = pl.pallas_call(
        functools.partial(dispatch_kernel, slot_cap),
        out_shape=(vmem_out((half, 2 * width)),) * 2,
        in_specs=[pl.BlockSpec(memory_space=pltpu.HBM)] * 6,
        out_specs=(vmem_whole,) * 2,
        scratch_shapes=[pltpu.VMEM(a.shape, a.dtype) for a in arguments] + [pltpu.SemaphoreType.DMA((6,))],
        compiler_params=params(16),
        name="dispatch",
    )(*[in_hbm(a) for a in arguments])
    got = swap(other, "expert", 1)

    arrived = []
    for m in range(chips):
        span = slice(m * slot_cap, (m + 1) * slot_cap)
        rows = jnp.concatenate([own[span], got[span]], axis=0)
        if Z3 and m == chips - 1:
            rows = join([rows], [arrived[1]])
        arrived.append(rows if m == 0 else swap(rows, "expert", 2 * m))

    quarter = chips // 4
    chunks = [[[q * quarter + i for q in quarters for i in range(quarter)] for quarters in c] for c in CHUNKS]
    chunk_count = len(chunks)
    returned = [None] * chips
    all_rows, all_hidden, all_pre = [], [], []
    steps = groups.bit_length() - 1
    weights = pl.pallas_call(
        load_kernel,
        out_shape=(vmem_out(win.shape), vmem_out(wout.shape)),
        in_specs=[pl.BlockSpec(memory_space=pltpu.HBM)] * 2 + [anywhere],
        out_specs=(vmem_whole,) * 2,
        scratch_shapes=[pltpu.SemaphoreType.DMA((2,))],
        compiler_params=params(16),
        cost_estimate=cost(0, int(C_LOAD * 8 * width * hidden_total)),
        name="load",
    )(in_hbm(win), in_hbm(wout), got if LOAD is None else arrived[LOAD * quarter])
    sums_of = []
    all_count = block * chips * groups
    weight_call = dict(
        in_specs=[vmem_whole] * (2 * chunk_count) + [anywhere],
        out_specs=(vmem_whole,) * 2,
        compiler_params=params(40),
        cost_estimate=cost(int(C_W * 2 * all_count * width * hidden_total), int(C_W * 2 * width * hidden_total)),
    )

    def weight_in_call(after):
        return pl.pallas_call(
            functools.partial(weight_in_kernel, chunk_count, width),
            out_shape=(jax.ShapeDtypeStruct((width, hidden_total), bf16), vmem_out((16, 128))),
            name="weight_in_grad",
            **weight_call,
        )(*all_rows, *all_pre, after)

    def weight_out_call(after):
        return pl.pallas_call(
            functools.partial(weight_out_kernel, chunk_count, width),
            out_shape=(jax.ShapeDtypeStruct((hidden_total, width), bf16), vmem_out((16, 128))),
            name="weight_out_grad",
            **weight_call,
        )(*all_rows, *all_hidden, after)

    deferred = []
    for number, chunk in enumerate(chunks):
        moved, places, start = [], [], 0
        for group in chunk:
            held = [jnp.concatenate([arrived[m] for m in group], axis=0)]
            size = held[0].shape[0]
            if HOLD and number:
                held = [join(held, early)]
            if EARLY_LOAD and not number and group is chunk[-1]:
                held = [join(held, weights[:1])]
            if FIRST_LOAD and not number and group is chunk[0]:
                held = [join(held, weights[:1])]
            if HOLD2 and number:
                held = [join(held, first[1 : HOLD2 + 1])]
            for step in range(steps):
                after = [arrived[m] for group in chunks[-1] for m in group] if WAIT_Z and not number and step else []
                both = join(held, after) if after else jnp.concatenate(held, axis=0)
                held.append(swap_groups(both, 1 << step))
            early = [held[1]]
            if not number and group is chunk[0]:
                first = held
            moved += held
            places += [(start, size, 0)] + [(start, size, 1 << step) for step in range(steps)]
            start += size
        inside = [m for group in chunk for m in group]
        count = len(inside) * block
        total = groups * count
        if DIRECT[number]:
            levels = [(p, p + 1) for p in range(1, groups)]
        else:
            levels = [(1 << step, 2 << step) for step in reversed(range(steps))]
        outs = pl.pallas_call(
            functools.partial(chunk_kernel, TILE, groups, levels, places),
            out_shape=tuple(vmem_out(((high - low) * count, width)) for low, high in levels)
            + (
                vmem_out((count, width)),
                vmem_out((total, 2 * width)),
                vmem_out((total, hidden_total)),
                vmem_out((total, hidden_total)),
            ),
            in_specs=[vmem_whole] * (len(moved) + 2) + [anywhere],
            out_specs=(vmem_whole,) * (len(levels) + 4),
            scratch_shapes=[pltpu.VMEM((total, width), f32)],
            compiler_params=params(32),
            cost_estimate=cost(int(C_CHUNK * 6 * total * width * hidden_total), int(C_CHUNK * 4 * width * hidden_total), int(C_CHUNK * total * hidden_total)),
            name="chunk",
        )(*moved, *weights, deferred[-1][-1] if deferred and IN_TURN else weights[0])
        sends, (kept, rows_all, hidden, pre) = outs[:-4], outs[-4:]
        all_rows.append(rows_all)
        all_hidden.append(hidden)
        all_pre.append(pre)
        deferred.append((inside, count, levels, sends, kept))

    def first_send(number):
        _, _, levels, sends, _ = deferred[number]
        return swap_groups(sends[0], levels[0][0])

    def rest(number, first, after):
        _, count, levels, sends, kept = deferred[number]
        parts = [first]
        for (low, high), value in zip(levels[1:], sends[1:], strict=True):
            if not DIRECT[number]:
                value = add_rows([value] + [part[low * count : high * count] for part in parts], after)
            parts.append(swap_groups(value, low))
        return [kept] + [part if part.shape[0] == count else part[:count] for part in parts]

    last = len(chunks) - 1
    firsts = [first_send(number) for number in range(last + 1)]
    kept_last = deferred[last][-1]
    after = {0: deferred[0][-1], 1: kept_last, 3: firsts[last]}.get(DEFER)
    if after is None:
        terms = rest(last, firsts[last], kept_last)
        after = terms[-1]
    for number in range(last):
        others = rest(number, firsts[number], after)
        sums_of.append(sum(t.astype(f32) for t in others).astype(bf16))
    if DEFER != 4:
        terms = rest(last, firsts[last], kept_last)
    grad_in, done = weight_in_call({0: sums_of[0], -1: kept_last}.get(W_AFTER, terms[W_AFTER]))
    sums_of.append(add_rows(terms, done))
    for (inside, *_), summed in zip(deferred, sums_of, strict=True):
        if Z1LAST and summed is not sums_of[-1]:
            summed = join([summed], sums_of[-1:])
        for i, m in enumerate(inside):
            piece = summed[i * block : (i + 1) * block]
            returned[m] = piece if m == 0 else swap(piece, "expert", 2 * m)

    grad_out, done = weight_out_call(sums_of[-1])
    back_own, for_partner = pl.pallas_call(
        functools.partial(pack_kernel, slot_cap),
        out_shape=(vmem_out((half, width)),) * 2,
        in_specs=[vmem_whole] * chips + [anywhere],
        out_specs=(vmem_whole,) * 2,
        compiler_params=params(16),
        name="pack",
    )(*returned, done)
    back_other = swap(for_partner, "expert", 1)
    input_grad = pl.pallas_call(
        functools.partial(combine_kernel, slot_cap),
        out_shape=jax.ShapeDtypeStruct((token_count, width), bf16),
        in_specs=[vmem_whole] * 5,
        out_specs=vmem_whole,
        compiler_params=params(16),
        name="combine",
    )(back_own, back_other, ids, slots, keep)
    return (input_grad, grad_in[None], grad_out[None])


def solution(mesh):
    tokens = P(("dp", "expert"), None)
    in_specs = (tokens,) * 6 + (P("expert", None, "dp"), P("expert", "dp", None))
    out_specs = (tokens, P("expert", None, "dp"), P("expert", "dp", None))
    return jax.shard_map(body, mesh=mesh, in_specs=in_specs, out_specs=out_specs, check_vma=False)
```

```python
import functools

import jax
import jax.numpy as jnp
from jax import lax
from jax.experimental import pallas as pl
from jax.experimental.pallas import tpu as pltpu
from jax.sharding import PartitionSpec as P

root_coef = 0.7978845608028654
cube_coef = 0.044715
vmem_whole = pl.BlockSpec(memory_space=pltpu.VMEM)
anywhere = pl.BlockSpec(memory_space=pl.ANY)
f32 = jnp.float32
CHUNKS = (((0,), (1,)), ((2,), (3,)))
DIRECT = (False, True)
TILE = 1280
C_CHUNK = 1.0
C_LOAD = 0.01
C_W = 0.01
LOAD = None
WAIT_Z = False
DEFER = 3
HOLD = False
EARLY_LOAD = False
Z1LAST = False
W_AFTER = -1
IN_TURN = True
UP = False
FIRST_SEND = True
FIRST_LOAD = True
HOLD2 = 0
Z3 = False
bf16 = jnp.bfloat16


def in_hbm(value):
    return pltpu.with_memory_space_constraint(value, pltpu.HBM)


def vmem_out(shape, dtype=bf16):
    return pltpu.VMEM(shape, dtype)


def params(mib):
    return pltpu.CompilerParams(vmem_limit_bytes=mib * 1024 * 1024)


def cost(flops, moved, trans=0):
    return pl.CostEstimate(flops=flops, bytes_accessed=moved, transcendentals=trans)


def selector_columns(ids, slots, keep, me, slot_cap, half):
    relative = ids ^ me
    column = (relative & 1) * half + (relative >> 1) * slot_cap + slots
    return jnp.where(keep > 0, column, -1)


def dispatch_kernel(slot_cap, *refs):
    sources, (own_ref, other_ref), held, sem = refs[:6], refs[6:8], refs[8:14], refs[14]
    copies = [pltpu.make_async_copy(a, b, sem.at[i]) for i, (a, b) in enumerate(zip(sources, held, strict=True))]
    for copy in copies:
        copy.start()
    for copy in copies:
        copy.wait()
    tokens_ref, grads_ref, gate_ref, ids_ref, slots_ref, keep_ref = held
    half = own_ref.shape[0]
    token_count, width = tokens_ref.shape
    me = lax.axis_index("expert")
    column = selector_columns(ids_ref[...], slots_ref[...], keep_ref[...], me, slot_cap, half)
    gate = gate_ref[...]
    for base, out_ref in ((half, other_ref), (0, own_ref)):
        rows = lax.broadcasted_iota(jnp.int32, (half, token_count), 0) + base
        first, second = rows == column[0:1], rows == column[1:2]
        picked = (first | second).astype(f32).astype(bf16)
        scale = jnp.sum(
            jnp.where(first, gate[0:1], 0.0) + jnp.where(second, gate[1:2], 0.0), axis=1, keepdims=True
        )
        out_ref[:, :width] = jnp.dot(picked, tokens_ref[...], preferred_element_type=f32).astype(bf16)
        row_grad = jnp.dot(picked, grads_ref[...], preferred_element_type=f32)
        out_ref[:, width:] = (scale * row_grad).astype(bf16)


def combine_kernel(slot_cap, own_ref, other_ref, ids_ref, slots_ref, keep_ref, out_ref):
    half = own_ref.shape[0]
    token_count = out_ref.shape[0]
    me = lax.axis_index("expert")
    column = selector_columns(ids_ref[...], slots_ref[...], keep_ref[...], me, slot_cap, half)
    total = jnp.zeros(out_ref.shape, f32)
    for base, rows_ref in ((0, own_ref), (half, other_ref)):
        rows = lax.broadcasted_iota(jnp.int32, (half, token_count), 0) + base
        picked = ((rows == column[0:1]) | (rows == column[1:2])).astype(f32).astype(bf16)
        total += lax.dot_general(picked, rows_ref[...], (((0,), (0,)), ((), ())), preferred_element_type=f32)
    out_ref[...] = total.astype(bf16)


def load_kernel(*refs):
    sources, targets, sem = refs[:2], refs[-3:-1], refs[-1]
    copies = [pltpu.make_async_copy(a, b, sem.at[i]) for i, (a, b) in enumerate(zip(sources, targets, strict=True))]
    for copy in copies:
        copy.start()
    for copy in copies:
        copy.wait()


def chunk_kernel(tile, groups, levels, places, *refs):
    moved, refs = refs[: len(places)], refs[len(places) :]
    (win_ref, wout_ref), outs = refs[:2], refs[3:]
    sends, kept_ref = outs[:-5], outs[-5]
    rows_ref, hidden_ref, pre_ref, acc_ref = outs[-4:]
    width, hidden_total = win_ref.shape
    count = rows_ref.shape[0] // groups
    for ref, (start, size, first) in zip(moved, places, strict=True):
        for i in range(ref.shape[0] // size):
            at = (first + i) * count + start
            rows_ref[at : at + size, :] = ref[i * size : (i + 1) * size, :]
    for base in range(0, hidden_total, tile):
        cols = slice(base, base + tile)
        preact = jnp.dot(rows_ref[:, :width], win_ref[:, cols], preferred_element_type=f32)
        backprop = lax.dot_general(
            rows_ref[:, width:], wout_ref[cols, :], (((1,), (1,)), ((), ())), preferred_element_type=f32
        )
        square = preact * preact
        tanh_value = jnp.tanh(root_coef * (preact + cube_coef * preact * square))
        one_plus = 0.5 * (1.0 + tanh_value)
        hidden_ref[:, cols] = (preact * one_plus).astype(bf16)
        slope = one_plus + 0.5 * preact * (1.0 - tanh_value * tanh_value) * (
            root_coef + (3.0 * cube_coef * root_coef) * square
        )
        grad_pre = (slope * backprop).astype(bf16)
        pre_ref[:, cols] = grad_pre
        term = lax.dot_general(
            grad_pre, win_ref[:, cols], (((1,), (1,)), ((), ())), preferred_element_type=f32
        )
        if base == 0:
            acc_ref[...] = term
        else:
            acc_ref[...] += term
    kept_ref[...] = acc_ref[:count, :].astype(bf16)
    for (low, high), ref in zip(levels, sends, strict=True):
        ref[...] = acc_ref[low * count : high * count, :].astype(bf16)


def stacked(refs, cols):
    return jnp.concatenate([ref[:, cols] for ref in refs], axis=0)


def weight_in_kernel(count, width, *refs):
    rows, pre = stacked(refs[:count], slice(0, width)), stacked(refs[count : 2 * count], slice(None))
    out_ref, done_ref = refs[-2:]
    total = lax.dot_general(rows, pre, (((0,), (0,)), ((), ())), preferred_element_type=f32)
    out_ref[...] = total.astype(bf16)
    done_ref[...] = jnp.zeros(done_ref.shape, bf16)


def weight_out_kernel(count, width, *refs):
    cot = stacked(refs[:count], slice(width, 2 * width))
    hidden = stacked(refs[count : 2 * count], slice(None))
    out_ref, done_ref = refs[-2:]
    total = lax.dot_general(hidden, cot, (((0,), (0,)), ((), ())), preferred_element_type=f32)
    out_ref[...] = total.astype(bf16)
    done_ref[...] = jnp.zeros(done_ref.shape, bf16)


def join_kernel(count, *refs):
    start = 0
    for ref in refs[:count]:
        refs[-1][start : start + ref.shape[0], :] = ref[...]
        start += ref.shape[0]


def join(values, after):
    rows = sum(v.shape[0] for v in values)
    return pl.pallas_call(
        functools.partial(join_kernel, len(values)),
        out_shape=vmem_out((rows, values[0].shape[1])),
        in_specs=[vmem_whole] * len(values) + [anywhere] * len(after),
        out_specs=vmem_whole,
        compiler_params=params(16),
        name="join",
    )(*values, *after)


def add_rows(values, after):
    return pl.pallas_call(
        sum_kernel,
        out_shape=vmem_out(values[0].shape),
        in_specs=[vmem_whole] * len(values) + [anywhere],
        out_specs=vmem_whole,
        compiler_params=params(16),
        name="sum",
    )(*values, after)


def sum_kernel(*refs):
    total = refs[0][...].astype(f32)
    for ref in refs[1:-2]:
        total = total + ref[...].astype(f32)
    refs[-1][...] = total.astype(bf16)


def pack_kernel(slot_cap, *refs):
    returned, (own_ref, other_ref) = refs[:-3], refs[-2:]
    rows = jnp.concatenate([ref[...].astype(f32) for ref in returned], axis=0)
    rows = rows.reshape(len(returned), 2, slot_cap, rows.shape[-1])
    for part, ref in ((0, own_ref), (1, other_ref)):
        ref[...] = rows[:, part].reshape(ref.shape).astype(bf16)


def swap(value, axis, offset):
    size = lax.axis_size(axis)
    return lax.ppermute(value, axis, [(i, i ^ offset) for i in range(size)])


def swap_groups(value, position):
    groups, owners = lax.axis_size("dp"), lax.axis_size("expert")
    bits = [1 << i for i in range(groups.bit_length() - 1)]
    offsets = [sum(b for i, b in enumerate(order) if position >> i & 1) for order in (bits, bits[::-1])]
    pairs = [(d * owners + e, (d ^ offsets[e & 1]) * owners + e) for d in range(groups) for e in range(owners)]
    return lax.ppermute(value, ("dp", "expert"), pairs)


def body(
    layer_input,
    output_grad,
    gate_weights,
    expert_ids,
    slot_positions,
    keep_mask,
    weight_in,
    weight_out,
):
    token_count, width = layer_input.shape
    owners = lax.axis_size("expert")
    groups = lax.axis_size("dp")
    slot_cap = 3 * token_count // (2 * owners)
    chips = owners // 2
    half = chips * slot_cap
    block = 2 * slot_cap
    gate, ids, slots, keep = gate_weights.T, expert_ids.T, slot_positions.T, keep_mask.T
    win, wout = weight_in[0], weight_out[0]
    hidden_total = win.shape[1]

    arguments = (layer_input, output_grad, gate, ids, slots, keep)
    own, other = pl.pallas_call(
        functools.partial(dispatch_kernel, slot_cap),
        out_shape=(vmem_out((half, 2 * width)),) * 2,
        in_specs=[pl.BlockSpec(memory_space=pltpu.HBM)] * 6,
        out_specs=(vmem_whole,) * 2,
        scratch_shapes=[pltpu.VMEM(a.shape, a.dtype) for a in arguments] + [pltpu.SemaphoreType.DMA((6,))],
        compiler_params=params(16),
        name="dispatch",
    )(*[in_hbm(a) for a in arguments])
    got = swap(other, "expert", 1)

    arrived = []
    for m in range(chips):
        span = slice(m * slot_cap, (m + 1) * slot_cap)
        rows = jnp.concatenate([own[span], got[span]], axis=0)
        if Z3 and m == chips - 1:
            rows = join([rows], [arrived[1]])
        arrived.append(rows if m == 0 else swap(rows, "expert", 2 * m))

    quarter = chips // 4
    chunks = [[[q * quarter + i for q in quarters for i in range(quarter)] for quarters in c] for c in CHUNKS]
    chunk_count = len(chunks)
    returned = [None] * chips
    all_rows, all_hidden, all_pre = [], [], []
    steps = groups.bit_length() - 1
    weights = pl.pallas_call(
        load_kernel,
        out_shape=(vmem_out(win.shape), vmem_out(wout.shape)),
        in_specs=[pl.BlockSpec(memory_space=pltpu.HBM)] * 2 + [anywhere],
        out_specs=(vmem_whole,) * 2,
        scratch_shapes=[pltpu.SemaphoreType.DMA((2,))],
        compiler_params=params(16),
        cost_estimate=cost(0, int(C_LOAD * 8 * width * hidden_total)),
        name="load",
    )(in_hbm(win), in_hbm(wout), got if LOAD is None else arrived[LOAD * quarter])
    sums_of = []
    all_count = block * chips * groups
    weight_call = dict(
        in_specs=[vmem_whole] * (2 * chunk_count) + [anywhere],
        out_specs=(vmem_whole,) * 2,
        compiler_params=params(40),
        cost_estimate=cost(int(C_W * 2 * all_count * width * hidden_total), int(C_W * 2 * width * hidden_total)),
    )

    def weight_in_call(after):
        return pl.pallas_call(
            functools.partial(weight_in_kernel, chunk_count, width),
            out_shape=(jax.ShapeDtypeStruct((width, hidden_total), bf16), vmem_out((16, 128))),
            name="weight_in_grad",
            **weight_call,
        )(*all_rows, *all_pre, after)

    def weight_out_call(after):
        return pl.pallas_call(
            functools.partial(weight_out_kernel, chunk_count, width),
            out_shape=(jax.ShapeDtypeStruct((hidden_total, width), bf16), vmem_out((16, 128))),
            name="weight_out_grad",
            **weight_call,
        )(*all_rows, *all_hidden, after)

    deferred = []
    for number, chunk in enumerate(chunks):
        moved, places, start = [], [], 0
        for group in chunk:
            held = [jnp.concatenate([arrived[m] for m in group], axis=0)]
            size = held[0].shape[0]
            if HOLD and number:
                held = [join(held, early)]
            if EARLY_LOAD and not number and group is chunk[-1]:
                held = [join(held, weights[:1])]
            if FIRST_LOAD and not number and group is chunk[0]:
                held = [join(held, weights[:1])]
            if HOLD2 and number:
                held = [join(held, first[1 : HOLD2 + 1])]
            for step in range(steps):
                after = [arrived[m] for group in chunks[-1] for m in group] if WAIT_Z and not number and step else []
                both = join(held, after) if after else jnp.concatenate(held, axis=0)
                held.append(swap_groups(both, 1 << step))
            early = [held[1]]
            if not number and group is chunk[0]:
                first = held
            moved += held
            places += [(start, size, 0)] + [(start, size, 1 << step) for step in range(steps)]
            start += size
        inside = [m for group in chunk for m in group]
        count = len(inside) * block
        total = groups * count
        if DIRECT[number]:
            levels = [(p, p + 1) for p in (range(1, groups) if UP else reversed(range(1, groups)))]
        else:
            levels = [(1 << step, 2 << step) for step in reversed(range(steps))]
        outs = pl.pallas_call(
            functools.partial(chunk_kernel, TILE, groups, levels, places),
            out_shape=tuple(vmem_out(((high - low) * count, width)) for low, high in levels)
            + (
                vmem_out((count, width)),
                vmem_out((total, 2 * width)),
                vmem_out((total, hidden_total)),
                vmem_out((total, hidden_total)),
            ),
            in_specs=[vmem_whole] * (len(moved) + 2) + [anywhere],
            out_specs=(vmem_whole,) * (len(levels) + 4),
            scratch_shapes=[pltpu.VMEM((total, width), f32)],
            compiler_params=params(32),
            cost_estimate=cost(int(C_CHUNK * 6 * total * width * hidden_total), int(C_CHUNK * 4 * width * hidden_total), int(C_CHUNK * total * hidden_total)),
            name="chunk",
        )(*moved, *weights, deferred[-1][-1] if deferred and IN_TURN else weights[0])
        sends, (kept, rows_all, hidden, pre) = outs[:-4], outs[-4:]
        all_rows.append(rows_all)
        all_hidden.append(hidden)
        all_pre.append(pre)
        deferred.append((inside, count, levels, sends, kept))

    def first_send(number):
        _, _, levels, sends, _ = deferred[number]
        return swap_groups(sends[0], levels[0][0])

    def rest(number, first, after):
        _, count, levels, sends, kept = deferred[number]
        parts = [first]
        for (low, high), value in zip(levels[1:], sends[1:], strict=True):
            if not DIRECT[number]:
                value = add_rows([value] + [part[low * count : high * count] for part in parts], after)
            parts.append(swap_groups(value, low))
        return [kept] + [part if part.shape[0] == count else part[:count] for part in parts]

    last = len(chunks) - 1
    firsts = [first_send(number) for number in range(last + 1)]
    kept_last = deferred[last][-1]
    after = {0: deferred[0][-1], 1: kept_last, 3: firsts[last]}.get(DEFER)
    if after is None:
        terms = rest(last, firsts[last], kept_last)
        after = terms[-1]
    for number in range(last):
        others = rest(number, firsts[number], after)
        sums_of.append(sum(t.astype(f32) for t in others).astype(bf16))
    if DEFER != 4:
        terms = rest(last, firsts[last], kept_last)
    grad_in, done = weight_in_call({0: sums_of[0], -1: kept_last}.get(W_AFTER, terms[W_AFTER]))
    sums_of.append(add_rows(terms, done))
    for (inside, *_), summed in zip(deferred, sums_of, strict=True):
        if Z1LAST and summed is not sums_of[-1]:
            summed = join([summed], sums_of[-1:])
        for i, m in enumerate(inside):
            piece = summed[i * block : (i + 1) * block]
            returned[m] = piece if m == 0 else swap(piece, "expert", 2 * m)

    grad_out, done = weight_out_call(sums_of[-1])
    back_own, for_partner = pl.pallas_call(
        functools.partial(pack_kernel, slot_cap),
        out_shape=(vmem_out((half, width)),) * 2,
        in_specs=[vmem_whole] * chips + [anywhere],
        out_specs=(vmem_whole,) * 2,
        compiler_params=params(16),
        name="pack",
    )(*returned, done)
    back_other = swap(for_partner, "expert", 1)
    input_grad = pl.pallas_call(
        functools.partial(combine_kernel, slot_cap),
        out_shape=jax.ShapeDtypeStruct((token_count, width), bf16),
        in_specs=[vmem_whole] * 5,
        out_specs=vmem_whole,
        compiler_params=params(16),
        name="combine",
    )(back_own, back_other, ids, slots, keep)
    return (input_grad, grad_in[None], grad_out[None])


def solution(mesh):
    tokens = P(("dp", "expert"), None)
    in_specs = (tokens,) * 6 + (P("expert", None, "dp"), P("expert", "dp", None))
    out_specs = (tokens, P("expert", None, "dp"), P("expert", "dp", None))
    return jax.shard_map(body, mesh=mesh, in_specs=in_specs, out_specs=out_specs, check_vma=False)
```

```python
import functools

import jax
import jax.numpy as jnp
from jax import lax
from jax.experimental import pallas as pl
from jax.experimental.pallas import tpu as pltpu
from jax.sharding import PartitionSpec as P

root_coef = 0.7978845608028654
cube_coef = 0.044715
vmem_whole = pl.BlockSpec(memory_space=pltpu.VMEM)
anywhere = pl.BlockSpec(memory_space=pl.ANY)
f32 = jnp.float32
CHUNKS = (((0,), (1,)), ((2,), (3,)))
DIRECT = (False, True)
TILE = 1280
C_CHUNK = 1.0
C_LOAD = 0.01
C_W = 0.01
LOAD = None
WAIT_Z = False
DEFER = 3
HOLD = False
EARLY_LOAD = False
Z1LAST = False
W_AFTER = -1
IN_TURN = True
UP = False
FIRST_SEND = True
FIRST_LOAD = True
HOLD2 = 0
Z3 = False
bf16 = jnp.bfloat16


def in_hbm(value):
    return pltpu.with_memory_space_constraint(value, pltpu.HBM)


def vmem_out(shape, dtype=bf16):
    return pltpu.VMEM(shape, dtype)


def params(mib):
    return pltpu.CompilerParams(vmem_limit_bytes=mib * 1024 * 1024)


def cost(flops, moved, trans=0):
    return pl.CostEstimate(flops=flops, bytes_accessed=moved, transcendentals=trans)


def selector_columns(ids, slots, keep, me, slot_cap, half):
    relative = ids ^ me
    column = (relative & 1) * half + (relative >> 1) * slot_cap + slots
    return jnp.where(keep > 0, column, -1)


def dispatch_kernel(slot_cap, *refs):
    sources, (own_ref, other_ref), held, sem = refs[:6], refs[6:8], refs[8:14], refs[14]
    copies = [pltpu.make_async_copy(a, b, sem.at[i]) for i, (a, b) in enumerate(zip(sources, held, strict=True))]
    for copy in copies:
        copy.start()
    for copy in copies:
        copy.wait()
    tokens_ref, grads_ref, gate_ref, ids_ref, slots_ref, keep_ref = held
    half = own_ref.shape[0]
    token_count, width = tokens_ref.shape
    me = lax.axis_index("expert")
    column = selector_columns(ids_ref[...], slots_ref[...], keep_ref[...], me, slot_cap, half)
    gate = gate_ref[...]
    for base, out_ref in ((half, other_ref), (0, own_ref)):
        rows = lax.broadcasted_iota(jnp.int32, (half, token_count), 0) + base
        first, second = rows == column[0:1], rows == column[1:2]
        picked = (first | second).astype(f32).astype(bf16)
        scale = jnp.sum(
            jnp.where(first, gate[0:1], 0.0) + jnp.where(second, gate[1:2], 0.0), axis=1, keepdims=True
        )
        out_ref[:, :width] = jnp.dot(picked, tokens_ref[...], preferred_element_type=f32).astype(bf16)
        row_grad = jnp.dot(picked, grads_ref[...], preferred_element_type=f32)
        out_ref[:, width:] = (scale * row_grad).astype(bf16)


def combine_kernel(slot_cap, own_ref, other_ref, ids_ref, slots_ref, keep_ref, out_ref):
    half = own_ref.shape[0]
    token_count = out_ref.shape[0]
    me = lax.axis_index("expert")
    column = selector_columns(ids_ref[...], slots_ref[...], keep_ref[...], me, slot_cap, half)
    total = jnp.zeros(out_ref.shape, f32)
    for base, rows_ref in ((0, own_ref), (half, other_ref)):
        rows = lax.broadcasted_iota(jnp.int32, (half, token_count), 0) + base
        picked = ((rows == column[0:1]) | (rows == column[1:2])).astype(f32).astype(bf16)
        total += lax.dot_general(picked, rows_ref[...], (((0,), (0,)), ((), ())), preferred_element_type=f32)
    out_ref[...] = total.astype(bf16)


def load_kernel(*refs):
    sources, targets, sem = refs[:2], refs[-3:-1], refs[-1]
    copies = [pltpu.make_async_copy(a, b, sem.at[i]) for i, (a, b) in enumerate(zip(sources, targets, strict=True))]
    for copy in copies:
        copy.start()
    for copy in copies:
        copy.wait()


def chunk_kernel(tile, groups, levels, places, *refs):
    moved, refs = refs[: len(places)], refs[len(places) :]
    (win_ref, wout_ref), outs = refs[:2], refs[3:]
    sends, kept_ref = outs[:-5], outs[-5]
    rows_ref, hidden_ref, pre_ref, acc_ref = outs[-4:]
    width, hidden_total = win_ref.shape
    count = rows_ref.shape[0] // groups
    for ref, (start, size, first) in zip(moved, places, strict=True):
        for i in range(ref.shape[0] // size):
            at = (first + i) * count + start
            rows_ref[at : at + size, :] = ref[i * size : (i + 1) * size, :]
    for base in range(0, hidden_total, tile):
        cols = slice(base, base + tile)
        preact = jnp.dot(rows_ref[:, :width], win_ref[:, cols], preferred_element_type=f32)
        backprop = lax.dot_general(
            rows_ref[:, width:], wout_ref[cols, :], (((1,), (1,)), ((), ())), preferred_element_type=f32
        )
        square = preact * preact
        tanh_value = jnp.tanh(root_coef * (preact + cube_coef * preact * square))
        one_plus = 0.5 * (1.0 + tanh_value)
        hidden_ref[:, cols] = (preact * one_plus).astype(bf16)
        slope = one_plus + 0.5 * preact * (1.0 - tanh_value * tanh_value) * (
            root_coef + (3.0 * cube_coef * root_coef) * square
        )
        grad_pre = (slope * backprop).astype(bf16)
        pre_ref[:, cols] = grad_pre
        term = lax.dot_general(
            grad_pre, win_ref[:, cols], (((1,), (1,)), ((), ())), preferred_element_type=f32
        )
        if base == 0:
            acc_ref[...] = term
        else:
            acc_ref[...] += term
    kept_ref[...] = acc_ref[:count, :].astype(bf16)
    for (low, high), ref in zip(levels, sends, strict=True):
        ref[...] = acc_ref[low * count : high * count, :].astype(bf16)


def stacked(refs, cols):
    return jnp.concatenate([ref[:, cols] for ref in refs], axis=0)


def weight_in_kernel(count, width, *refs):
    rows, pre = stacked(refs[:count], slice(0, width)), stacked(refs[count : 2 * count], slice(None))
    out_ref, done_ref = refs[-2:]
    total = lax.dot_general(rows, pre, (((0,), (0,)), ((), ())), preferred_element_type=f32)
    out_ref[...] = total.astype(bf16)
    done_ref[...] = jnp.zeros(done_ref.shape, bf16)


def weight_out_kernel(count, width, part, *refs):
    out_ref, done_ref, held_ref, sem = refs[-4:]
    size = held_ref.shape[0]
    span = slice(part * size, (part + 1) * size)
    cot = stacked(refs[:count], slice(width, 2 * width))
    hidden = stacked(refs[count : 2 * count], span)
    total = lax.dot_general(hidden, cot, (((0,), (0,)), ((), ())), preferred_element_type=f32)
    held_ref[...] = total.astype(bf16)
    copy = pltpu.make_async_copy(held_ref, out_ref.at[span], sem)
    copy.start()
    done_ref[...] = jnp.zeros(done_ref.shape, bf16)
    copy.wait()


def join_kernel(count, *refs):
    start = 0
    for ref in refs[:count]:
        refs[-1][start : start + ref.shape[0], :] = ref[...]
        start += ref.shape[0]


def join(values, after):
    rows = sum(v.shape[0] for v in values)
    return pl.pallas_call(
        functools.partial(join_kernel, len(values)),
        out_shape=vmem_out((rows, values[0].shape[1])),
        in_specs=[vmem_whole] * len(values) + [anywhere] * len(after),
        out_specs=vmem_whole,
        compiler_params=params(16),
        name="join",
    )(*values, *after)


def add_rows(values, after):
    return pl.pallas_call(
        sum_kernel,
        out_shape=vmem_out(values[0].shape),
        in_specs=[vmem_whole] * len(values) + [anywhere],
        out_specs=vmem_whole,
        compiler_params=params(16),
        name="sum",
    )(*values, after)


def sum_kernel(*refs):
    total = refs[0][...].astype(f32)
    for ref in refs[1:-2]:
        total = total + ref[...].astype(f32)
    refs[-1][...] = total.astype(bf16)


def pack_kernel(slot_cap, *refs):
    returned, (own_ref, other_ref) = refs[:-3], refs[-2:]
    rows = jnp.concatenate([ref[...].astype(f32) for ref in returned], axis=0)
    rows = rows.reshape(len(returned), 2, slot_cap, rows.shape[-1])
    for part, ref in ((0, own_ref), (1, other_ref)):
        ref[...] = rows[:, part].reshape(ref.shape).astype(bf16)


def swap(value, axis, offset):
    size = lax.axis_size(axis)
    return lax.ppermute(value, axis, [(i, i ^ offset) for i in range(size)])


def swap_groups(value, position):
    groups, owners = lax.axis_size("dp"), lax.axis_size("expert")
    bits = [1 << i for i in range(groups.bit_length() - 1)]
    offsets = [sum(b for i, b in enumerate(order) if position >> i & 1) for order in (bits, bits[::-1])]
    pairs = [(d * owners + e, (d ^ offsets[e & 1]) * owners + e) for d in range(groups) for e in range(owners)]
    return lax.ppermute(value, ("dp", "expert"), pairs)


def body(
    layer_input,
    output_grad,
    gate_weights,
    expert_ids,
    slot_positions,
    keep_mask,
    weight_in,
    weight_out,
):
    token_count, width = layer_input.shape
    owners = lax.axis_size("expert")
    groups = lax.axis_size("dp")
    slot_cap = 3 * token_count // (2 * owners)
    chips = owners // 2
    half = chips * slot_cap
    block = 2 * slot_cap
    gate, ids, slots, keep = gate_weights.T, expert_ids.T, slot_positions.T, keep_mask.T
    win, wout = weight_in[0], weight_out[0]
    hidden_total = win.shape[1]

    arguments = (layer_input, output_grad, gate, ids, slots, keep)
    own, other = pl.pallas_call(
        functools.partial(dispatch_kernel, slot_cap),
        out_shape=(vmem_out((half, 2 * width)),) * 2,
        in_specs=[pl.BlockSpec(memory_space=pltpu.HBM)] * 6,
        out_specs=(vmem_whole,) * 2,
        scratch_shapes=[pltpu.VMEM(a.shape, a.dtype) for a in arguments] + [pltpu.SemaphoreType.DMA((6,))],
        compiler_params=params(16),
        name="dispatch",
    )(*[in_hbm(a) for a in arguments])
    got = swap(other, "expert", 1)

    arrived = []
    for m in range(chips):
        span = slice(m * slot_cap, (m + 1) * slot_cap)
        rows = jnp.concatenate([own[span], got[span]], axis=0)
        if Z3 and m == chips - 1:
            rows = join([rows], [arrived[1]])
        arrived.append(rows if m == 0 else swap(rows, "expert", 2 * m))

    quarter = chips // 4
    chunks = [[[q * quarter + i for q in quarters for i in range(quarter)] for quarters in c] for c in CHUNKS]
    chunk_count = len(chunks)
    returned = [None] * chips
    all_rows, all_hidden, all_pre = [], [], []
    steps = groups.bit_length() - 1
    weights = pl.pallas_call(
        load_kernel,
        out_shape=(vmem_out(win.shape), vmem_out(wout.shape)),
        in_specs=[pl.BlockSpec(memory_space=pltpu.HBM)] * 2 + [anywhere],
        out_specs=(vmem_whole,) * 2,
        scratch_shapes=[pltpu.SemaphoreType.DMA((2,))],
        compiler_params=params(16),
        cost_estimate=cost(0, int(C_LOAD * 8 * width * hidden_total)),
        name="load",
    )(in_hbm(win), in_hbm(wout), got if LOAD is None else arrived[LOAD * quarter])
    sums_of = []
    all_count = block * chips * groups
    weight_call = dict(
        in_specs=[vmem_whole] * (2 * chunk_count) + [anywhere],
        out_specs=(vmem_whole,) * 2,
        compiler_params=params(40),
        cost_estimate=cost(int(C_W * 2 * all_count * width * hidden_total), int(C_W * 2 * width * hidden_total)),
    )

    def weight_in_call(after):
        return pl.pallas_call(
            functools.partial(weight_in_kernel, chunk_count, width),
            out_shape=(jax.ShapeDtypeStruct((width, hidden_total), bf16), vmem_out((16, 128))),
            name="weight_in_grad",
            **weight_call,
        )(*all_rows, *all_pre, after)

    def weight_out_call(part, after, prior=()):
        in_hbm_spec = pl.BlockSpec(memory_space=pltpu.HBM)
        operands = (*all_rows, *all_hidden, after, *prior)
        return pl.pallas_call(
            functools.partial(weight_out_kernel, chunk_count, width, part),
            out_shape=(jax.ShapeDtypeStruct((hidden_total, width), bf16), vmem_out((16, 128))),
            in_specs=[vmem_whole] * (2 * chunk_count) + [anywhere] + [in_hbm_spec] * len(prior),
            out_specs=(in_hbm_spec, vmem_whole),
            scratch_shapes=[pltpu.VMEM((hidden_total // 2, width), bf16), pltpu.SemaphoreType.DMA],
            input_output_aliases={len(operands) - 1: 0} if prior else {},
            compiler_params=params(40),
            cost_estimate=cost(int(C_W * all_count * width * hidden_total), int(C_W * width * hidden_total)),
            name="weight_out_grad",
        )(*operands)

    deferred = []
    for number, chunk in enumerate(chunks):
        moved, places, start = [], [], 0
        for group in chunk:
            held = [jnp.concatenate([arrived[m] for m in group], axis=0)]
            size = held[0].shape[0]
            if HOLD and number:
                held = [join(held, early)]
            if EARLY_LOAD and not number and group is chunk[-1]:
                held = [join(held, weights[:1])]
            if FIRST_LOAD and not number and group is chunk[0]:
                held = [join(held, weights[:1])]
            if HOLD2 and number:
                held = [join(held, first[1 : HOLD2 + 1])]
            for step in range(steps):
                after = [arrived[m] for group in chunks[-1] for m in group] if WAIT_Z and not number and step else []
                both = join(held, after) if after else jnp.concatenate(held, axis=0)
                held.append(swap_groups(both, 1 << step))
            early = [held[1]]
            if not number and group is chunk[0]:
                first = held
            moved += held
            places += [(start, size, 0)] + [(start, size, 1 << step) for step in range(steps)]
            start += size
        inside = [m for group in chunk for m in group]
        count = len(inside) * block
        total = groups * count
        if DIRECT[number]:
            levels = [(p, p + 1) for p in (range(1, groups) if UP else reversed(range(1, groups)))]
        else:
            levels = [(1 << step, 2 << step) for step in reversed(range(steps))]
        outs = pl.pallas_call(
            functools.partial(chunk_kernel, TILE, groups, levels, places),
            out_shape=tuple(vmem_out(((high - low) * count, width)) for low, high in levels)
            + (
                vmem_out((count, width)),
                vmem_out((total, 2 * width)),
                vmem_out((total, hidden_total)),
                vmem_out((total, hidden_total)),
            ),
            in_specs=[vmem_whole] * (len(moved) + 2) + [anywhere],
            out_specs=(vmem_whole,) * (len(levels) + 4),
            scratch_shapes=[pltpu.VMEM((total, width), f32)],
            compiler_params=params(32),
            cost_estimate=cost(int(C_CHUNK * 6 * total * width * hidden_total), int(C_CHUNK * 4 * width * hidden_total), int(C_CHUNK * total * hidden_total)),
            name="chunk",
        )(*moved, *weights, deferred[-1][-1] if deferred and IN_TURN else weights[0])
        sends, (kept, rows_all, hidden, pre) = outs[:-4], outs[-4:]
        all_rows.append(rows_all)
        all_hidden.append(hidden)
        all_pre.append(pre)
        deferred.append((inside, count, levels, sends, kept))

    def first_send(number):
        _, _, levels, sends, _ = deferred[number]
        return swap_groups(sends[0], levels[0][0])

    def rest(number, first, after):
        _, count, levels, sends, kept = deferred[number]
        parts = [first]
        for (low, high), value in zip(levels[1:], sends[1:], strict=True):
            if not DIRECT[number]:
                value = add_rows([value] + [part[low * count : high * count] for part in parts], after)
            parts.append(swap_groups(value, low))
        return [kept] + [part if part.shape[0] == count else part[:count] for part in parts]

    last = len(chunks) - 1
    firsts = [first_send(number) for number in range(last + 1)]
    kept_last = deferred[last][-1]
    after = {0: deferred[0][-1], 1: kept_last, 3: firsts[last]}.get(DEFER)
    if after is None:
        terms = rest(last, firsts[last], kept_last)
        after = terms[-1]
    for number in range(last):
        others = rest(number, firsts[number], after)
        sums_of.append(sum(t.astype(f32) for t in others).astype(bf16))
    if DEFER != 4:
        terms = rest(last, firsts[last], kept_last)
    grad_in, done = weight_in_call({0: sums_of[0], -1: kept_last}.get(W_AFTER, terms[W_AFTER]))
    half_out, done = weight_out_call(0, done)
    sums_of.append(add_rows(terms, done))
    for (inside, *_), summed in zip(deferred, sums_of, strict=True):
        if Z1LAST and summed is not sums_of[-1]:
            summed = join([summed], sums_of[-1:])
        for i, m in enumerate(inside):
            piece = summed[i * block : (i + 1) * block]
            returned[m] = piece if m == 0 else swap(piece, "expert", 2 * m)

    grad_out, done = weight_out_call(1, sums_of[-1], (half_out,))
    back_own, for_partner = pl.pallas_call(
        functools.partial(pack_kernel, slot_cap),
        out_shape=(vmem_out((half, width)),) * 2,
        in_specs=[vmem_whole] * chips + [anywhere],
        out_specs=(vmem_whole,) * 2,
        compiler_params=params(16),
        name="pack",
    )(*returned, done)
    back_other = swap(for_partner, "expert", 1)
    input_grad = pl.pallas_call(
        functools.partial(combine_kernel, slot_cap),
        out_shape=jax.ShapeDtypeStruct((token_count, width), bf16),
        in_specs=[vmem_whole] * 5,
        out_specs=vmem_whole,
        compiler_params=params(16),
        name="combine",
    )(back_own, back_other, ids, slots, keep)
    return (input_grad, grad_in[None], grad_out[None])


def solution(mesh):
    tokens = P(("dp", "expert"), None)
    in_specs = (tokens,) * 6 + (P("expert", None, "dp"), P("expert", "dp", None))
    out_specs = (tokens, P("expert", None, "dp"), P("expert", "dp", None))
    return jax.shard_map(body, mesh=mesh, in_specs=in_specs, out_specs=out_specs, check_vma=False)
```
